32 devices in a mesh: ctx: 8 (over y, x, core), mem: 4 (over z).
Axes of the slice: x: 2, y: 2, z: 4, core: 2. Of those that a mesh axis runs over, the one named last changes fastest.
Arguments:
- queries: bfloat16 [4096, 1024], P(('ctx', 'mem')), may hold values from -6 to 6
- key_vectors: bfloat16 [4096, 1024], P(('ctx', 'mem')), may hold values from -30 to 30
- value_vectors: bfloat16 [4096, 1024], P(('ctx', 'mem')), may hold values from -30 to 30
- log_decay: bfloat16 [4096, 16], P(('ctx', 'mem')), may hold values from -1 to 0
- routes: int32 [4096, 2], P(('ctx', 'mem')), may hold values from 0 to 3, all different within a row; in each aligned block of 128 rows (0 to 127, 128 to 255, ...) at most 96 rows name the same one
- route_weight: float32 [4096, 2], P(('ctx', 'mem')), may hold values from 0.2 to 1
- out_gain: float32 [1024], replicated, may hold values from 0.5 to 1.5
Outputs:
- mixed_out: bfloat16 [4096, 1024], P(('ctx', 'mem'))
The draws below stay inside these ranges and needn't reach their ends.
Inputs may be any that keep to these rules, and one draw needn't show every extreme that they name: `routes`: each token names 2 different memories; among the 128 tokens of one device (aligned blocks) no memory is named more than 96 times, and in every draw some memory is named exactly 96 times.
All inputs are finite; a program needn't handle non-finite values.
Results may differ from the reference program's by a relative error of at most 0.0046.
Values may be sent and summed in bfloat16 or wider, within the bound.
A program may use at most 128 MiB of HBM per device.

```python
import math
import jax
import jax.numpy as jnp
import numpy as np
from jax import lax

ATTN_SUBSET = 16
DH = 64
TOP = 2
TOK_DEV = 128
MEMS = 4
CAP = 96
SBLK = 256
SEQ_SPAN_COUNT = 4096
GROUP_TOK = 512


def group_level(key):
    level_key = jax.random.fold_in(key, 911)
    pieces = jax.random.split(level_key, 3)
    group_count = SEQ_SPAN_COUNT // GROUP_TOK
    loud_group = jax.random.uniform(pieces[0], (group_count,)) < 0.34
    loud_level = jax.random.uniform(pieces[1], (group_count,), minval=1.4, maxval=2.0)
    quiet_level = jax.random.uniform(pieces[2], (group_count,), minval=-3.2, maxval=-2.6)
    level = jnp.exp(jnp.where(loud_group, loud_level, quiet_level))
    return jnp.repeat(level, GROUP_TOK)


def leveled_draw(key, salt):
    level = group_level(key)
    entry_key = jax.random.fold_in(key, salt)
    shape = (SEQ_SPAN_COUNT, ATTN_SUBSET * DH)
    base = jnp.clip(jax.random.normal(entry_key, shape), -4.0, 4.0)
    return (base * level[:, None]).astype(jnp.float32).astype(jnp.bfloat16)


def draw_key_vectors(key, part):
    return leveled_draw(key, 1)


def draw_value_vectors(key, part):
    return leveled_draw(key, 2)


def draw_log_decay(key, part):
    keys = jax.random.split(key, 8)
    fast_count = 3 * ATTN_SUBSET // 16
    middle_count = 5 * ATTN_SUBSET // 16
    head_order = jax.random.permutation(keys[0], ATTN_SUBSET)
    rapid_store = head_order < fast_count
    middle_store = (head_order >= fast_count) & (head_order < fast_count + middle_count)
    fast_len = jax.random.uniform(keys[1], (ATTN_SUBSET,), minval=30.0, maxval=50.0)
    keep = jax.random.uniform(keys[2], (ATTN_SUBSET,), minval=0.5, maxval=0.85)
    phase = jax.random.uniform(keys[3], (ATTN_SUBSET,), minval=0.0, maxval=6.283)
    store_slots_list = jax.random.randint(keys[4], (2,), 0, SEQ_SPAN_COUNT)
    objective_numbers = jax.random.uniform(keys[5], (2, ATTN_SUBSET), minval=0.5, maxval=0.8)
    group_fade = jax.random.uniform(keys[7], (ATTN_SUBSET,), minval=7.1, maxval=7.9)
    jitter = jnp.exp(0.15 * jnp.clip(jax.random.normal(keys[6], (SEQ_SPAN_COUNT, ATTN_SUBSET)), -2.0, 2.0))
    present_spot = jnp.arange(SEQ_SPAN_COUNT, dtype=jnp.int32)
    wave = jnp.exp(0.7 * jnp.sin(6.283 * 3.0 * present_spot[:, None].astype(jnp.float32) / SEQ_SPAN_COUNT + phase[None, :]))
    slow_forget_factor = jnp.log(keep)[None, :] / SEQ_SPAN_COUNT * wave * jitter
    rapid_forget_factor = -wave * jitter / fast_len[None, :]
    middle_forget_factor = -jitter * group_fade[None, :] / GROUP_TOK
    spike_extent = jnp.zeros((SEQ_SPAN_COUNT, ATTN_SUBSET), jnp.float32)
    for step_ordinal in range(2):
        spike_extent = spike_extent + jnp.where(present_spot[:, None] == store_slots_list[step_ordinal], jnp.log(objective_numbers[step_ordinal])[None, :], 0.0)
    forget_factor = jnp.where(rapid_store[None, :], rapid_forget_factor, jnp.where(middle_store[None, :], middle_forget_factor, slow_forget_factor + spike_extent))
    forget_factor = jnp.clip(forget_factor, -1.0, 0.0)
    return forget_factor.astype(jnp.float32).astype(jnp.bfloat16)


def block_levels(rng, dims, cuts, least, largest):
    def one(dim, parts):
        steps = jax.random.uniform(jax.random.fold_in(jax.random.fold_in(rng, 6), dim), (parts,), jnp.float32, least / len(cuts), largest / len(cuts))
        return jnp.repeat(jnp.exp(steps), dims[dim] // parts).reshape((-1,) + (1,) * (len(dims) - dim - 1))

    loudness = one(*cuts[0])
    for cut in cuts[1:]:
        loudness = loudness * one(*cut)
    return loudness


def routed_block(key, own, number, rows, count, top, bound, slope):
    order = jax.random.permutation(key, count)
    packed, common = load_shares(count, rows * top, bound, slope, True), load_shares(count, rows * top, bound, slope, False)
    places = jnp.arange(count)

    def named(tallies, offset_by):
        used = int((tallies > 0).sum())
        fixed = max(1, used // 4)
        shifted = fixed + (places - fixed + offset_by * (used - fixed)) % max(1, count - fixed)
        return jnp.zeros((count,), jnp.int32).at[order[jnp.where(places < fixed, places, shifted)]].set(jnp.asarray(tallies, jnp.int32))

    tallies = jnp.where(number % 4 == 0, named(packed, number // 4), named(common, number - number // 4 - 1))
    mixed = jax.random.permutation(jax.random.fold_in(own, 3), count)
    source_of, receiver = mixed[0:count // 2 * 2:2], mixed[1:count // 2 * 2:2]
    margin = jnp.minimum(tallies[source_of] - 1, bound - tallies[receiver]) // 2
    margin = jnp.where((source_of == order[0]) | (receiver == order[0]) | (tallies[receiver] == 0), 0, jnp.maximum(margin, 0))
    shifted = jax.random.randint(jax.random.fold_in(own, 4), (count // 2,), 0, 1 << 20) % (margin + 1)
    tallies = tallies.at[source_of].add(-shifted).at[receiver].add(shifted)
    members = jnp.searchsorted(jnp.cumsum(tallies), jnp.arange(rows * top), side="right").astype(jnp.int32)
    grid = members.reshape(top, rows).T
    grid = grid[jax.random.permutation(jax.random.fold_in(own, 1), rows)]
    offset_by = jax.random.randint(jax.random.fold_in(own, 2), (rows, 1), 0, top)
    return jnp.take_along_axis(grid, (jnp.arange(top)[None, :] + offset_by) % top, axis=1)


def load_shares(number_of, total, most, lean, full):
    portions = [(1 << 20) // math.isqrt(rank ** lean) + 1 for rank in range(1, number_of + 1)]
    largest = most if full else min(most, max(-(-total // number_of), total * portions[0] // sum(portions)))
    least = 1 if total - largest >= number_of - 1 else 0
    given, surplus = [largest] + [least] * (number_of - 1), total - largest - least * (number_of - 1)
    while surplus > 0:
        candidates = [i for i in range(1, number_of) if given[i] < largest] or [i for i in range(1, number_of) if given[i] < most]
        mass, budget = sum([portions[i] for i in candidates]), surplus
        for i in candidates:
            more = min(most - given[i], max(1, budget * portions[i] // mass), surplus)
            given[i] = given[i] + more
            surplus = surplus - more
    return np.array(given)


def bell_draw(key, dims, width, reach, cuts=(), kind=jnp.bfloat16):
    values = width * jax.random.normal(key, dims, jnp.float32)
    if cuts:
        values = values * block_levels(key, dims, cuts, -0.22, 0.18)
    return jnp.clip(values, -reach, reach).astype(kind)


def setup_inputs(seed: int = 0) -> dict:
    streams_of = jax.random.split(jax.random.key(seed), 8)
    queries = bell_draw(streams_of[0], (SEQ_SPAN_COUNT, ATTN_SUBSET * DH), 1.0, 6.0, ((0, 32),))
    key_vectors = draw_key_vectors(jax.random.fold_in(streams_of[7], 71), 0)
    value_vectors = draw_value_vectors(jax.random.fold_in(streams_of[7], 71), 0)
    log_decay = draw_log_decay(jax.random.fold_in(streams_of[7], 71), 0)
    routes_keys = jax.random.split(jax.random.fold_in(streams_of[4], 1), SEQ_SPAN_COUNT // TOK_DEV)
    routes_turns = jax.random.permutation(jax.random.fold_in(streams_of[4], 3), SEQ_SPAN_COUNT // TOK_DEV)
    routes = jax.vmap(lambda own, number: routed_block(jax.random.fold_in(streams_of[4], 2), own, number, TOK_DEV, MEMS, TOP, CAP, 2))(routes_keys, routes_turns).reshape((SEQ_SPAN_COUNT, TOP))
    route_weight = jnp.clip(0.2 + 0.8 * jax.random.uniform(streams_of[5], (SEQ_SPAN_COUNT, TOP), jnp.float32) ** block_levels(streams_of[5], (SEQ_SPAN_COUNT, TOP), ((0, 32),), -0.2, 0.2), 0.2, 1.0)
    out_gain = jnp.clip(1.0 + 0.1 * jax.random.normal(streams_of[6], (ATTN_SUBSET * DH,), jnp.float32), 0.5, 1.5)
    return {"queries": queries, "key_vectors": key_vectors, "value_vectors": value_vectors, "log_decay": log_decay, "routes": routes, "route_weight": route_weight, "out_gain": out_gain}


precise = lax.Precision.HIGHEST

def block_run(query_blk, key_blk, value_blk, decay_blk):
    head_count = query_blk.shape[2]
    head_size = query_blk.shape[3]

    def advance(state, pieces):
        query_now, key_now, value_now, decay_now = pieces
        cumul = jnp.cumsum(decay_now, axis=0)
        store_slots_list = jnp.arange(query_now.shape[0], dtype=jnp.int32)
        causal = (store_slots_list[:, None] >= store_slots_list[None, :])[None]
        spread = jnp.transpose(cumul)[:, :, None] - jnp.transpose(cumul)[:, None, :]
        factor = jnp.where(causal, jnp.exp(jnp.where(causal, spread, 0.0)), 0.0)
        query_wide = query_now.astype(jnp.float32)
        value_wide = value_now.astype(jnp.float32)
        scores = jnp.einsum('lhd,shd->hls', query_wide, key_now.astype(jnp.float32))
        weights = lax.optimization_barrier((scores * factor).astype(jnp.bfloat16)).astype(jnp.float32)
        inner = jnp.einsum('hls,shd->lhd', weights, value_wide)
        outer = jnp.einsum('lhd,hde->lhe', query_wide * jnp.exp(cumul)[:, :, None], state, precision=precise)
        last = cumul[-1]
        faded = key_now.astype(jnp.float32) * jnp.exp(last[None, :] - cumul)[:, :, None]
        state = jnp.exp(last)[:, None, None] * state + jnp.einsum('lhd,lhe->hde', faded, value_wide, precision=precise)
        return (state, inner + outer)
    start = jnp.zeros((head_count, head_size, head_size), jnp.float32)
    final_state, outputs = lax.scan(advance, start, (query_blk, key_blk, value_blk, decay_blk))
    return outputs

def reference(queries, key_vectors, value_vectors, log_decay, routes, route_weight, out_gain):
    tok_total = queries.shape[0]
    query_heads = queries.reshape(tok_total, ATTN_SUBSET, DH)
    key_heads = key_vectors.reshape(tok_total, ATTN_SUBSET, DH)
    value_heads = value_vectors.reshape(tok_total, ATTN_SUBSET, DH)
    decay = log_decay.astype(jnp.float32)
    block_count = tok_total // SBLK
    shared = block_run(query_heads.reshape(block_count, SBLK, ATTN_SUBSET, DH), key_heads.reshape(block_count, SBLK, ATTN_SUBSET, DH), value_heads.reshape(block_count, SBLK, ATTN_SUBSET, DH), decay.reshape(block_count, SBLK, ATTN_SUBSET))
    shared = lax.optimization_barrier(shared.reshape(tok_total, ATTN_SUBSET, DH).astype(jnp.bfloat16)).astype(jnp.float32)
    dev_count = tok_total // TOK_DEV
    mem_ids = jnp.arange(MEMS, dtype=jnp.int32)
    member = routes[:, :, None] == mem_ids[None, None, :]
    assign = lax.optimization_barrier(jnp.sum(member.astype(jnp.int32), axis=1)).astype(jnp.int32)
    blocked = assign.reshape(dev_count, TOK_DEV, MEMS)
    ranked = (jnp.cumsum(blocked, axis=1).astype(jnp.int32) - blocked).reshape(tok_total, MEMS)
    owner_dev = (jnp.arange(tok_total, dtype=jnp.int32) // TOK_DEV).astype(jnp.int32)
    position = (owner_dev[:, None] * CAP + ranked).astype(jnp.int32)
    slot_total = dev_count * CAP
    span = SBLK // TOK_DEV * CAP

    def per_memory(total, memory):
        chosen = assign[:, memory] == 1
        where_to = jnp.where(chosen, position[:, memory], slot_total).astype(jnp.int32)

        def placed(array):
            empty = jnp.zeros((slot_total,) + array.shape[1:], array.dtype)
            return empty.at[where_to].set(array, mode='drop')
        slot_q = placed(query_heads).reshape(slot_total // span, span, ATTN_SUBSET, DH)
        slot_k = placed(key_heads).reshape(slot_total // span, span, ATTN_SUBSET, DH)
        slot_v = placed(value_heads).reshape(slot_total // span, span, ATTN_SUBSET, DH)
        slot_g = placed(decay).reshape(slot_total // span, span, ATTN_SUBSET)
        routed = block_run(slot_q, slot_k, slot_v, slot_g).reshape(slot_total, ATTN_SUBSET, DH)
        routed = lax.optimization_barrier(routed.astype(jnp.bfloat16)).astype(jnp.float32)
        picked = routed[jnp.minimum(where_to, slot_total - 1)]
        share = lax.optimization_barrier(jnp.sum(jnp.where(member[:, :, memory], route_weight, 0.0), axis=1))
        return (total + share[:, None, None] * picked, None)
    routed_sum, leftover = lax.scan(per_memory, jnp.zeros((tok_total, ATTN_SUBSET, DH), jnp.float32), mem_ids)
    combined = shared + routed_sum
    scale = lax.rsqrt(lax.optimization_barrier(jnp.mean(combined * combined, axis=-1, keepdims=True)) + 1e-06)
    result = combined * scale * out_gain.reshape(ATTN_SUBSET, DH)
    return result.astype(jnp.bfloat16).reshape(tok_total, ATTN_SUBSET * DH)
```

```python
import functools

import jax
import jax.numpy as jnp
from jax import lax
from jax.experimental import pallas as pl
from jax.experimental.pallas import tpu as pltpu
from jax.sharding import PartitionSpec as P

MESH = pl.DeviceIdType.MESH
GROUP = 8
NT = (((1,), (1,)), ((), ()))
TN = (((0,), (0,)), ((), ()))


def mm(a, b, dims=(((1,), (0,)), ((), ()))):
    return lax.dot_general(a, b, dims, preferred_element_type=jnp.float32)


def halves(x):
    high = x.astype(jnp.bfloat16)
    return high, (x - high.astype(jnp.float32)).astype(jnp.bfloat16)


def kernel(
    n_ctx, n_mem, n_heads, pad,
    q_ref, k_ref, v_ref, small_ref, gain_ref, out_ref,
    qbuf, kbuf, vbuf, tab_mine, tab, vt_buf, t_buf, fade_buf, pre_buf, inner_buf, send_buf,
    total_buf, keep_buf,
    send_sem, recv_sem, out_send, out_recv, tot_send, tot_recv,
):
    slots = n_mem + 1
    groups = n_ctx * n_mem // GROUP
    tok = q_ref.shape[0]
    half = 64
    me = lax.axis_index("ctx") * n_mem + lax.axis_index("mem")
    group = lax.div(me, GROUP)
    rank = lax.rem(me, GROUP)

    def device(block):
        return (lax.div(block, n_mem), lax.rem(block, n_mem))

    def peer(j):
        return lax.rem(rank + j, GROUP)

    def source(j):
        return lax.rem(rank + (GROUP - j), GROUP)

    def other(j):
        return lax.rem(group + j, groups)

    def origin(j):
        return lax.rem(group + (groups - j), groups)

    barrier = pltpu.get_barrier_semaphore()

    def greet(j, _):
        pl.semaphore_signal(
            barrier, inc=1, device_id=device(group * GROUP + peer(j)), device_id_type=MESH
        )
        return 0

    def greet_group(j, _):
        pl.semaphore_signal(
            barrier, inc=1, device_id=device(other(j) * GROUP + rank), device_id_type=MESH
        )
        return 0

    lax.fori_loop(1, GROUP, greet, 0)
    lax.fori_loop(1, groups, greet_group, 0)

    decay = small_ref[0:n_heads, :]
    first, second = small_ref[n_heads : n_heads + 1, :], small_ref[n_heads + 1 : n_heads + 2, :]
    w_first = small_ref[n_heads + 2 : n_heads + 3, :]
    w_second = small_ref[n_heads + 3 : n_heads + 4, :]
    row = lax.broadcasted_iota(jnp.int32, (tok, tok), 0)
    col = lax.broadcasted_iota(jnp.int32, (tok, tok), 1)
    causal = row <= col
    upper = jnp.where(causal, 1.0, 0.0).astype(jnp.bfloat16)
    tab_mine[...] = jnp.zeros_like(tab_mine)
    for m in range(slots):
        if m == 0:
            masked, weight = decay, jnp.ones_like(w_first)
        else:
            in_first, in_second = first == float(m - 1), second == float(m - 1)
            masked = jnp.where(in_first | in_second, decay, 0.0)
            weight = jnp.where(in_first, w_first, jnp.where(in_second, w_second, 0.0))
        cumul = mm(masked.astype(jnp.bfloat16), upper)
        for p in range(GROUP):
            for h in range(2):
                tab_mine[p, h * pad + m : h * pad + m + 1, :] = cumul[2 * p + h : 2 * p + h + 1, :]
            tab_mine[p, 2 * pad + m : 2 * pad + m + 1, :] = weight

    pl.semaphore_wait(barrier, GROUP - 1 + groups - 1)

    def columns(ref, r):
        return ref.at[:, pl.ds(pl.multiple_of(r * 128, 128), 128)]

    def transfer(kind, j, to, slot_of):
        src, dst = {
            0: lambda: (tab_mine.at[to], tab.at[slot_of]),
            1: lambda: (columns(k_ref, to), kbuf.at[slot_of]),
            2: lambda: (columns(v_ref, to), vbuf.at[slot_of]),
            3: lambda: (columns(q_ref, to), qbuf.at[slot_of]),
        }[kind]()
        return pltpu.make_async_remote_copy(
            src_ref=src,
            dst_ref=dst,
            send_sem=send_sem.at[kind, j],
            recv_sem=recv_sem.at[kind, j],
            device_id=device(group * GROUP + to),
            device_id_type=MESH,
        )

    for kind in range(4):

        def launch(j, _, kind=kind):
            transfer(kind, j, peer(j), rank).start()
            return 0

        lax.fori_loop(1, GROUP, launch, 0)

    tab[rank] = tab_mine[rank]
    own = pl.ds(pl.multiple_of(rank * 128, 128), 128)
    kbuf[rank] = k_ref[:, own]
    vbuf[rank] = v_ref[:, own]
    qbuf[rank] = q_ref[:, own]

    left = lax.broadcasted_iota(jnp.int32, (1, 128), 1) < half

    def factors(i):
        weight = tab[i, 2 * pad : 3 * pad, :]
        return [(tab[i, h * pad : (h + 1) * pad, :], weight) for h in range(2)]

    def gather_state(j, _):
        i = source(j)

        @pl.when(j > 0)
        def _():
            for kind in range(3):
                transfer(kind, j, peer(j), rank).wait_recv()

        keys = kbuf[i]
        vt = vbuf[i].astype(jnp.float32).T
        vt_buf[i] = vt.astype(jnp.bfloat16)
        parts, fades = [], []
        for h, (cumul, weight) in enumerate(factors(i)):
            last = cumul[:, tok - 1 : tok]
            faded = jnp.where(weight > 0.0, jnp.exp(last - cumul), 0.0)
            mine = vt[h * half : (h + 1) * half, :]
            scaled = jnp.concatenate([mine * faded[m : m + 1, :] for m in range(slots)], axis=0)
            parts.append(mm(scaled.astype(jnp.bfloat16), keys))
            fades.append(jnp.broadcast_to(jnp.exp(last), (pad, 128)))
        t_buf[i] = jnp.where(left, parts[0], parts[1])
        fade_buf[i] = jnp.where(left, fades[0], fades[1])
        return 0

    lax.fori_loop(0, GROUP, gather_state, 0)

    for m in range(slots):
        rows = pl.ds(m * half, half)
        state = jnp.zeros((half, 128), jnp.float32)
        kept = jnp.ones((1, 128), jnp.float32)
        for i in range(GROUP):
            fade = fade_buf[i, m : m + 1, :]
            added = t_buf[i, rows, :]
            t_buf[i, rows, :] = state
            pre_buf[i, m : m + 1, :] = kept
            state = fade * state + added
            kept = kept * fade
        total_buf[group, rows, :] = state.astype(jnp.bfloat16)
        keep_buf[group, m : m + 1, :] = kept

    def exchange(j):
        to = device(other(j) * GROUP + rank)
        return [
            pltpu.make_async_remote_copy(
                src_ref=ref.at[group],
                dst_ref=ref.at[group],
                send_sem=tot_send.at[kind, j],
                recv_sem=tot_recv.at[kind, j],
                device_id=to,
                device_id_type=MESH,
            )
            for kind, ref in enumerate((total_buf, keep_buf))
        ]

    def launch_totals(j, _):
        for copy in exchange(j):
            copy.start()
        return 0

    lax.fori_loop(1, groups, launch_totals, 0)

    def two_heads(i):
        queries = qbuf[i]
        zero = jnp.zeros_like(queries)
        return jnp.concatenate(
            [jnp.where(left, queries, zero), jnp.where(left, zero, queries)], axis=0
        )

    def inside(j, _):
        i = source(j)

        @pl.when(j > 0)
        def _():
            transfer(3, j, peer(j), rank).wait_recv()

        scores = mm(kbuf[i], two_heads(i), NT)
        for h, (cumul, weight) in enumerate(factors(i)):
            middle = 0.5 * cumul[:, tok - 1 : tok]
            read_hi, read_lo = halves(weight * jnp.exp(cumul - middle))
            write_hi, write_lo = halves(jnp.where(weight > 0.0, jnp.exp(middle - cumul), 0.0))
            factor = mm(
                jnp.concatenate([write_hi, write_lo, write_hi], axis=0),
                jnp.concatenate([read_hi, read_hi, read_lo], axis=0),
                TN,
            )
            part = scores[:, h * tok : (h + 1) * tok] * factor
            part = jnp.where(causal, part, 0.0).astype(jnp.bfloat16)
            inner_buf[i, :, h * tok : (h + 1) * tok] = mm(
                vt_buf[i, h * half : (h + 1) * half, :], part
            )
        return 0

    lax.fori_loop(0, GROUP, inside, 0)

    def await_totals(j, _):
        for copy in exchange(j):
            copy.wait_recv()
        return 0

    lax.fori_loop(1, groups, await_totals, 0)

    def carry(g, state):
        parts = []
        for m in range(slots):
            before = state[m * half : (m + 1) * half, :]
            new = keep_buf[g, m : m + 1, :] * before + total_buf[
                g, m * half : (m + 1) * half, :
            ].astype(jnp.float32)
            parts.append(jnp.where(g < group, new, before))
        return jnp.concatenate(parts, axis=0)

    carried = lax.fori_loop(0, groups, carry, jnp.zeros((slots * half, 128), jnp.float32))
    gain = gain_ref[rank]

    def give_back(j):
        to = peer(j)
        return pltpu.make_async_remote_copy(
            src_ref=send_buf.at[to],
            dst_ref=columns(out_ref, rank),
            send_sem=out_send.at[j],
            recv_sem=out_recv.at[j],
            device_id=device(group * GROUP + to),
            device_id_type=MESH,
        )

    def finish(step, _):
        j = GROUP - 1 - step
        i = peer(j)
        state = jnp.concatenate(
            [
                t_buf[i, m * half : (m + 1) * half, :]
                + pre_buf[i, m : m + 1, :] * carried[m * half : (m + 1) * half, :]
                for m in range(slots)
            ],
            axis=0,
        )
        read = mm(state.astype(jnp.bfloat16), two_heads(i), NT)
        level = jnp.concatenate(
            [weight * jnp.exp(cumul) for cumul, weight in factors(i)], axis=1
        )
        total = inner_buf[i]
        for m in range(slots):
            total = total + level[m : m + 1, :] * read[m * half : (m + 1) * half, :]
        scale = lax.rsqrt(jnp.mean(total * total, axis=0, keepdims=True) + 1e-06)
        normed = total * scale
        flat = jnp.concatenate([normed[:, :tok], normed[:, tok:]], axis=0)
        send_buf[i] = (flat.T * gain).astype(jnp.bfloat16)

        @pl.when(j > 0)
        def _():
            give_back(j).start()

        return 0

    lax.fori_loop(0, GROUP, finish, 0)
    out_ref[:, own] = send_buf[rank]

    def drain(j, _):
        for kind in range(4):
            transfer(kind, j, peer(j), rank).wait_send()
        copy = give_back(j)
        copy.wait_send()
        copy.wait_recv()
        return 0

    lax.fori_loop(1, GROUP, drain, 0)

    def drain_totals(j, _):
        for copy in exchange(j):
            copy.wait_send()
        return 0

    lax.fori_loop(1, groups, drain_totals, 0)


def on_device(queries, key_vectors, value_vectors, log_decay, routes, route_weight, out_gain):
    n_ctx, n_mem = lax.axis_size("ctx"), lax.axis_size("mem")
    tok, width = queries.shape
    heads = log_decay.shape[1]
    groups = n_ctx * n_mem // GROUP
    slots = n_mem + 1
    pad = (slots + 7) // 8 * 8
    small = jnp.concatenate(
        [
            log_decay.astype(jnp.float32),
            routes.astype(jnp.float32),
            route_weight,
            jnp.zeros((tok, 4), jnp.float32),
        ],
        axis=1,
    ).T
    gain = out_gain.reshape(GROUP, 1, 128)
    vmem = pl.BlockSpec(memory_space=pltpu.VMEM)
    return pl.pallas_call(
        functools.partial(kernel, n_ctx, n_mem, heads, pad),
        out_shape=jax.ShapeDtypeStruct((tok, width), jnp.bfloat16),
        in_specs=[vmem] * 5,
        out_specs=vmem,
        scratch_shapes=[
            pltpu.VMEM((GROUP, tok, 128), jnp.bfloat16),
            pltpu.VMEM((GROUP, tok, 128), jnp.bfloat16),
            pltpu.VMEM((GROUP, tok, 128), jnp.bfloat16),
            pltpu.VMEM((GROUP, 3 * pad, tok), jnp.float32),
            pltpu.VMEM((GROUP, 3 * pad, tok), jnp.float32),
            pltpu.VMEM((GROUP, 128, tok), jnp.bfloat16),
            pltpu.VMEM((GROUP, slots * 64, 128), jnp.float32),
            pltpu.VMEM((GROUP, pad, 128), jnp.float32),
            pltpu.VMEM((GROUP, pad, 128), jnp.float32),
            pltpu.VMEM((GROUP, 64, 2 * tok), jnp.float32),
            pltpu.VMEM((GROUP, tok, 128), jnp.bfloat16),
            pltpu.VMEM((groups, slots * 64, 128), jnp.bfloat16),
            pltpu.VMEM((groups, pad, 128), jnp.float32),
            pltpu.SemaphoreType.DMA((4, GROUP)),
            pltpu.SemaphoreType.DMA((4, GROUP)),
            pltpu.SemaphoreType.DMA((GROUP,)),
            pltpu.SemaphoreType.DMA((GROUP,)),
            pltpu.SemaphoreType.DMA((2, groups)),
            pltpu.SemaphoreType.DMA((2, groups)),
        ],
        compiler_params=pltpu.CompilerParams(
            collective_id=0, has_side_effects=True, vmem_limit_bytes=48 * 1024 * 1024
        ),
        cost_estimate=pl.CostEstimate(
            flops=2 * GROUP * 128 * 128 * 128 * 20, bytes_accessed=4 << 20, transcendentals=0
        ),
    )(queries, key_vectors, value_vectors, small, gain)


def solution(mesh):
    rows = P(("ctx", "mem"), None)
    return jax.shard_map(
        on_device,
        mesh=mesh,
        in_specs=(rows, rows, rows, rows, rows, rows, P()),
        out_specs=rows,
        check_vma=False,
    )
```

```python
import functools

import jax
import jax.numpy as jnp
from jax import lax
from jax.experimental import pallas as pl
from jax.experimental.pallas import tpu as pltpu
from jax.sharding import PartitionSpec as P

MESH = pl.DeviceIdType.MESH
GROUP = 8
NT = (((1,), (1,)), ((), ()))
TN = (((0,), (0,)), ((), ()))


def mm(a, b, dims=(((1,), (0,)), ((), ()))):
    return lax.dot_general(a, b, dims, preferred_element_type=jnp.float32)


def halves(x):
    high = x.astype(jnp.bfloat16)
    return high, (x - high.astype(jnp.float32)).astype(jnp.bfloat16)


def kernel(
    n_ctx, n_mem, n_heads, pad,
    q_ref, k_ref, v_ref, decay_ref, routes_ref, weight_ref, gain_ref, out_ref,
    qbuf, kbuf, vbuf, tab_mine, tab, vt_buf, t_buf, fade_buf, pre_buf, inner_buf, send_buf,
    total_buf, keep_buf, decay_buf, routes_buf, weight_buf, gain_buf,
    send_sem, recv_sem, out_send, out_recv, tot_send, tot_recv, own_sem, small_sem,
):
    slots = n_mem + 1
    groups = n_ctx * n_mem // GROUP
    tok = q_ref.shape[0]
    half = 64
    me = lax.axis_index("ctx") * n_mem + lax.axis_index("mem")
    group = lax.div(me, GROUP)
    rank = lax.rem(me, GROUP)

    def device(block):
        return (lax.div(block, n_mem), lax.rem(block, n_mem))

    def flipped(j):
        partner = rank
        for bit in (1, 2, 4):
            if j & bit:
                partner = partner + bit - 2 * bit * lax.rem(lax.div(rank, bit), 2)
        return partner

    peers = [flipped(j) for j in range(GROUP)]
    devices = [device(group * GROUP + r) for r in peers]

    def other(j):
        return lax.rem(group + j, groups)

    small = [
        pltpu.make_async_copy(src, dst, small_sem.at[i])
        for i, (src, dst) in enumerate(
            (
                (decay_ref, decay_buf),
                (routes_ref, routes_buf),
                (weight_ref, weight_buf),
                (gain_ref, gain_buf),
            )
        )
    ]
    for copy in small:
        copy.start()

    def columns(ref, r):
        return ref.at[:, pl.ds(pl.multiple_of(r * 128, 128), 128)]

    own = [
        pltpu.make_async_copy(columns(src, rank), dst.at[rank], own_sem.at[i])
        for i, (src, dst) in enumerate(((k_ref, kbuf), (v_ref, vbuf), (q_ref, qbuf)))
    ]
    for copy in own:
        copy.start()

    barrier = pltpu.get_barrier_semaphore()
    for j in range(1, GROUP):
        pl.semaphore_signal(barrier, inc=1, device_id=devices[j], device_id_type=MESH)

    def greet_group(j, _):
        pl.semaphore_signal(
            barrier, inc=1, device_id=device(other(j) * GROUP + rank), device_id_type=MESH
        )
        return 0

    lax.fori_loop(1, groups, greet_group, 0)

    row = lax.broadcasted_iota(jnp.int32, (tok, tok), 0)
    col = lax.broadcasted_iota(jnp.int32, (tok, tok), 1)
    causal = row <= col
    upper = jnp.where(causal, 1.0, 0.0).astype(jnp.bfloat16)
    tab_mine[...] = jnp.zeros_like(tab_mine)
    for copy in small:
        copy.wait()
    decay = decay_buf[...].astype(jnp.float32)
    first, second = routes_buf[0:1, :], routes_buf[1:2, :]
    w_first, w_second = weight_buf[0:1, :], weight_buf[1:2, :]
    for m in range(slots):
        if m == 0:
            masked, weight = decay, jnp.ones_like(w_first)
        else:
            in_first, in_second = first == m - 1, second == m - 1
            masked = jnp.where(in_first | in_second, decay, 0.0)
            weight = jnp.where(in_first, w_first, jnp.where(in_second, w_second, 0.0))
        cumul = mm(masked.astype(jnp.bfloat16), upper)
        for p in range(GROUP):
            for h in range(2):
                tab_mine[p, h * pad + m : h * pad + m + 1, :] = cumul[2 * p + h : 2 * p + h + 1, :]
            tab_mine[p, 2 * pad + m : 2 * pad + m + 1, :] = weight

    pl.semaphore_wait(barrier, GROUP - 1 + groups - 1)

    def transfer(kind, j):
        to = peers[j]
        src, dst = {
            0: lambda: (tab_mine.at[to], tab.at[rank]),
            1: lambda: (columns(k_ref, to), kbuf.at[rank]),
            2: lambda: (columns(v_ref, to), vbuf.at[rank]),
            3: lambda: (columns(q_ref, to), qbuf.at[rank]),
        }[kind]()
        return pltpu.make_async_remote_copy(
            src_ref=src,
            dst_ref=dst,
            send_sem=send_sem.at[kind, j],
            recv_sem=recv_sem.at[kind, j],
            device_id=devices[j],
            device_id_type=MESH,
        )

    far_first = (2, 6, 3, 7, 1, 5, 4)
    for kinds in ((0, 1, 2), (3,)):
        for j in far_first:
            for kind in kinds:
                transfer(kind, j).start()

    tab[rank] = tab_mine[rank]

    left = lax.broadcasted_iota(jnp.int32, (1, 128), 1) < half

    def split(x, axis):
        zero = jnp.zeros_like(x)
        return jnp.concatenate([jnp.where(left, x, zero), jnp.where(left, zero, x)], axis=axis)

    def factors(i):
        weight = tab[i, 2 * pad : 3 * pad, :]
        return [(tab[i, h * pad : (h + 1) * pad, :], weight) for h in range(2)]

    steps = ((0, 4), (1, 5), (2, 6), (3, 7))

    def gather_state(i):
        vt = vbuf[i].astype(jnp.float32).T
        vt_buf[i] = vt.astype(jnp.bfloat16)
        parts, fades = [], []
        for h, (cumul, weight) in enumerate(factors(i)):
            last = cumul[:, tok - 1 : tok]
            faded = jnp.where(weight > 0.0, jnp.exp(last - cumul), 0.0)
            mine = vt[h * half : (h + 1) * half, :]
            parts.append(
                jnp.concatenate([mine * faded[m : m + 1, :] for m in range(slots)], axis=0)
            )
            fades.append(jnp.broadcast_to(jnp.exp(last), (pad, 128)))
        scaled = jnp.concatenate(parts, axis=1).astype(jnp.bfloat16)
        t_buf[i] = mm(scaled, split(kbuf[i], 0))
        fade_buf[i] = jnp.where(left, fades[0], fades[1])

    for step in steps:
        for j in step:
            if j == 0:
                own[0].wait()
                own[1].wait()
            else:
                for kind in range(3):
                    transfer(kind, j).wait_recv()
        for j in step:
            gather_state(peers[j])

    for m in range(slots):
        rows = pl.ds(m * half, half)
        state = jnp.zeros((half, 128), jnp.float32)
        kept = jnp.ones((1, 128), jnp.float32)
        for i in range(GROUP):
            fade = fade_buf[i, m : m + 1, :]
            added = t_buf[i, rows, :]
            t_buf[i, rows, :] = state
            pre_buf[i, m : m + 1, :] = kept
            state = fade * state + added
            kept = kept * fade
        total_buf[group, rows, :] = state.astype(jnp.bfloat16)
        keep_buf[group, m : m + 1, :] = kept

    def exchange(j):
        to = device(other(j) * GROUP + rank)
        return [
            pltpu.make_async_remote_copy(
                src_ref=ref.at[group],
                dst_ref=ref.at[group],
                send_sem=tot_send.at[kind, j],
                recv_sem=tot_recv.at[kind, j],
                device_id=to,
                device_id_type=MESH,
            )
            for kind, ref in enumerate((total_buf, keep_buf))
        ]

    def launch_totals(j, _):
        for copy in exchange(j):
            copy.start()
        return 0

    lax.fori_loop(1, groups, launch_totals, 0)

    def inside(i):
        scores = mm(kbuf[i], split(qbuf[i], 0), NT)
        for h, (cumul, weight) in enumerate(factors(i)):
            middle = 0.5 * cumul[:, tok - 1 : tok]
            read_hi, read_lo = halves(weight * jnp.exp(cumul - middle))
            write_hi, write_lo = halves(jnp.where(weight > 0.0, jnp.exp(middle - cumul), 0.0))
            factor = mm(
                jnp.concatenate([write_hi, write_lo, write_hi], axis=0),
                jnp.concatenate([read_hi, read_hi, read_lo], axis=0),
                TN,
            )
            part = scores[:, h * tok : (h + 1) * tok] * factor
            part = jnp.where(causal, part, 0.0).astype(jnp.bfloat16)
            inner_buf[i, :, h * tok : (h + 1) * tok] = mm(
                vt_buf[i, h * half : (h + 1) * half, :], part
            )

    for step in steps:
        for j in step:
            if j == 0:
                own[2].wait()
            else:
                transfer(3, j).wait_recv()
        for j in step:
            inside(peers[j])

    def await_totals(j, _):
        for copy in exchange(j):
            copy.wait_recv()
        return 0

    lax.fori_loop(1, groups, await_totals, 0)

    def carry(g, state):
        parts = []
        for m in range(slots):
            before = state[m * half : (m + 1) * half, :]
            new = keep_buf[g, m : m + 1, :] * before + total_buf[
                g, m * half : (m + 1) * half, :
            ].astype(jnp.float32)
            parts.append(jnp.where(g < group, new, before))
        return jnp.concatenate(parts, axis=0)

    carry_buf = jnp.zeros((slots * half, 128), jnp.float32)
    carried = lax.fori_loop(0, groups, carry, carry_buf)
    gain = gain_buf[rank]

    def give_back(j):
        return pltpu.make_async_remote_copy(
            src_ref=send_buf.at[peers[j]],
            dst_ref=columns(out_ref, rank),
            send_sem=out_send.at[j],
            recv_sem=out_recv.at[j],
            device_id=devices[j],
            device_id_type=MESH,
        )

    def finish(i):
        state = jnp.concatenate(
            [
                t_buf[i, m * half : (m + 1) * half, :]
                + pre_buf[i, m : m + 1, :] * carried[m * half : (m + 1) * half, :]
                for m in range(slots)
            ],
            axis=0,
        )
        read = mm(state.astype(jnp.bfloat16), split(qbuf[i], 0), NT)
        level = jnp.concatenate(
            [weight * jnp.exp(cumul) for cumul, weight in factors(i)], axis=1
        )
        total = inner_buf[i]
        for m in range(slots):
            total = total + level[m : m + 1, :] * read[m * half : (m + 1) * half, :]
        scale = lax.rsqrt(jnp.mean(total * total, axis=0, keepdims=True) + 1e-06)
        normed = total * scale
        flat = jnp.concatenate([normed[:, :tok], normed[:, tok:]], axis=0)
        send_buf[i] = (flat.T * gain).astype(jnp.bfloat16)

    for step in ((2, 6), (3, 7), (1, 5), (4, 0)):
        for j in step:
            finish(peers[j])
        for j in step:
            if j > 0:
                give_back(j).start()

    out_ref[:, pl.ds(pl.multiple_of(rank * 128, 128), 128)] = send_buf[rank]

    for j in range(1, GROUP):
        for kind in range(4):
            transfer(kind, j).wait_send()
        copy = give_back(j)
        copy.wait_send()
        copy.wait_recv()

    def drain_totals(j, _):
        for copy in exchange(j):
            copy.wait_send()
        return 0

    lax.fori_loop(1, groups, drain_totals, 0)


def on_device(queries, key_vectors, value_vectors, log_decay, routes, route_weight, out_gain):
    n_ctx, n_mem = lax.axis_size("ctx"), lax.axis_size("mem")
    tok, width = queries.shape
    heads = log_decay.shape[1]
    groups = n_ctx * n_mem // GROUP
    slots = n_mem + 1
    pad = (slots + 7) // 8 * 8
    gain = out_gain.reshape(GROUP, 1, 128)
    hbm = pl.BlockSpec(memory_space=pltpu.HBM)
    return pl.pallas_call(
        functools.partial(kernel, n_ctx, n_mem, heads, pad),
        out_shape=jax.ShapeDtypeStruct((tok, width), jnp.bfloat16),
        in_specs=[hbm] * 7,
        out_specs=pl.BlockSpec(memory_space=pltpu.VMEM),
        scratch_shapes=[
            pltpu.VMEM((GROUP, tok, 128), jnp.bfloat16),
            pltpu.VMEM((GROUP, tok, 128), jnp.bfloat16),
            pltpu.VMEM((GROUP, tok, 128), jnp.bfloat16),
            pltpu.VMEM((GROUP, 3 * pad, tok), jnp.float32),
            pltpu.VMEM((GROUP, 3 * pad, tok), jnp.float32),
            pltpu.VMEM((GROUP, 128, tok), jnp.bfloat16),
            pltpu.VMEM((GROUP, slots * 64, 128), jnp.float32),
            pltpu.VMEM((GROUP, pad, 128), jnp.float32),
            pltpu.VMEM((GROUP, pad, 128), jnp.float32),
            pltpu.VMEM((GROUP, 64, 2 * tok), jnp.float32),
            pltpu.VMEM((GROUP, tok, 128), jnp.bfloat16),
            pltpu.VMEM((groups, slots * 64, 128), jnp.bfloat16),
            pltpu.VMEM((groups, pad, 128), jnp.float32),
            pltpu.VMEM((heads, tok), jnp.bfloat16),
            pltpu.VMEM((2, tok), jnp.int32),
            pltpu.VMEM((2, tok), jnp.float32),
            pltpu.VMEM((GROUP, 1, 128), jnp.float32),
            pltpu.SemaphoreType.DMA((4, GROUP)),
            pltpu.SemaphoreType.DMA((4, GROUP)),
            pltpu.SemaphoreType.DMA((GROUP,)),
            pltpu.SemaphoreType.DMA((GROUP,)),
            pltpu.SemaphoreType.DMA((2, groups)),
            pltpu.SemaphoreType.DMA((2, groups)),
            pltpu.SemaphoreType.DMA((3,)),
            pltpu.SemaphoreType.DMA((4,)),
        ],
        compiler_params=pltpu.CompilerParams(
            collective_id=0, has_side_effects=True, vmem_limit_bytes=63 * 1024 * 1024
        ),
        cost_estimate=pl.CostEstimate(
            flops=2 * GROUP * 128 * 128 * 128 * 20, bytes_accessed=4 << 20, transcendentals=0
        ),
    )(queries, key_vectors, value_vectors, log_decay.T, routes.T, route_weight.T, gain)


def solution(mesh):
    rows = P(("ctx", "mem"), None)
    return jax.shard_map(
        on_device,
        mesh=mesh,
        in_specs=(rows, rows, rows, rows, rows, rows, P()),
        out_specs=rows,
        check_vma=False,
    )
```

```python
import functools

import jax
import jax.numpy as jnp
from jax import lax
from jax.experimental import pallas as pl
from jax.experimental.pallas import tpu as pltpu
from jax.sharding import PartitionSpec as P

MESH = pl.DeviceIdType.MESH
GROUP = 8
NT = (((1,), (1,)), ((), ()))
TN = (((0,), (0,)), ((), ()))


def mm(a, b, dims=(((1,), (0,)), ((), ()))):
    return lax.dot_general(a, b, dims, preferred_element_type=jnp.float32)


def halves(x):
    high = x.astype(jnp.bfloat16)
    return high, (x - high.astype(jnp.float32)).astype(jnp.bfloat16)


def kernel(
    n_ctx, n_mem, n_heads, pad,
    q_ref, k_ref, v_ref, decay_ref, routes_ref, weight_ref, gain_ref, out_ref,
    qbuf, kbuf, vbuf, tab_mine, tab, vt_buf, t_buf, fade_buf, pre_buf, inner_buf, send_buf,
    total_buf, keep_buf, decay_buf, routes_buf, weight_buf, gain_buf,
    send_sem, recv_sem, out_send, out_recv, tot_send, tot_recv, own_sem, small_sem,
):
    slots = n_mem + 1
    groups = n_ctx * n_mem // GROUP
    tok = q_ref.shape[0]
    half = 64
    me = lax.axis_index("ctx") * n_mem + lax.axis_index("mem")
    group = lax.div(me, GROUP)
    rank = lax.rem(me, GROUP)

    def device(block):
        return (lax.div(block, n_mem), lax.rem(block, n_mem))

    def flipped(j):
        partner = rank
        for bit in (1, 2, 4):
            if j & bit:
                partner = partner + bit - 2 * bit * lax.rem(lax.div(rank, bit), 2)
        return partner

    peers = [flipped(j) for j in range(GROUP)]
    devices = [device(group * GROUP + r) for r in peers]

    def other(j):
        return lax.rem(group + j, groups)

    small = [
        pltpu.make_async_copy(src, dst, small_sem.at[i])
        for i, (src, dst) in enumerate(
            (
                (decay_ref, decay_buf),
                (routes_ref, routes_buf),
                (weight_ref, weight_buf),
                (gain_ref, gain_buf),
            )
        )
    ]
    for copy in small:
        copy.start()

    def columns(ref, r):
        return ref.at[:, pl.ds(pl.multiple_of(r * 128, 128), 128)]

    own = [
        pltpu.make_async_copy(columns(src, rank), dst.at[rank], own_sem.at[i])
        for i, (src, dst) in enumerate(((k_ref, kbuf), (v_ref, vbuf), (q_ref, qbuf)))
    ]
    for copy in own:
        copy.start()

    barrier = pltpu.get_barrier_semaphore()
    for j in range(1, GROUP):
        pl.semaphore_signal(barrier, inc=1, device_id=devices[j], device_id_type=MESH)

    def greet_group(j, _):
        pl.semaphore_signal(
            barrier, inc=1, device_id=device(other(j) * GROUP + rank), device_id_type=MESH
        )
        return 0

    lax.fori_loop(1, groups, greet_group, 0)

    row = lax.broadcasted_iota(jnp.int32, (tok, tok), 0)
    col = lax.broadcasted_iota(jnp.int32, (tok, tok), 1)
    causal = row <= col
    upper = jnp.where(causal, 1.0, 0.0).astype(jnp.bfloat16)
    tab_mine[...] = jnp.zeros_like(tab_mine)
    for copy in small:
        copy.wait()
    decay = decay_buf[...].astype(jnp.float32)
    first, second = routes_buf[0:1, :], routes_buf[1:2, :]
    w_first, w_second = weight_buf[0:1, :], weight_buf[1:2, :]
    for m in range(slots):
        if m == 0:
            masked, weight = decay, jnp.ones_like(w_first)
        else:
            in_first, in_second = first == m - 1, second == m - 1
            masked = jnp.where(in_first | in_second, decay, 0.0)
            weight = jnp.where(in_first, w_first, jnp.where(in_second, w_second, 0.0))
        cumul = mm(masked.astype(jnp.bfloat16), upper)
        for p in range(GROUP):
            for h in range(2):
                tab_mine[p, h * pad + m : h * pad + m + 1, :] = cumul[2 * p + h : 2 * p + h + 1, :]
            tab_mine[p, 2 * pad + m : 2 * pad + m + 1, :] = weight

    pl.semaphore_wait(barrier, GROUP - 1 + groups - 1)

    def transfer(kind, j):
        to = peers[j]
        src, dst = {
            0: lambda: (tab_mine.at[to], tab.at[rank]),
            1: lambda: (columns(k_ref, to), kbuf.at[rank]),
            2: lambda: (columns(v_ref, to), vbuf.at[rank]),
            3: lambda: (columns(q_ref, to), qbuf.at[rank]),
        }[kind]()
        return pltpu.make_async_remote_copy(
            src_ref=src,
            dst_ref=dst,
            send_sem=send_sem.at[kind, j],
            recv_sem=recv_sem.at[kind, j],
            device_id=devices[j],
            device_id_type=MESH,
        )

    for kinds, order in (((0, 1, 2), (4, 2, 1, 6, 5, 3, 7)), ((3,), (2, 6, 3, 7, 1, 5, 4))):
        for j in order:
            for kind in kinds:
                transfer(kind, j).start()

    tab[rank] = tab_mine[rank]

    left = lax.broadcasted_iota(jnp.int32, (1, 128), 1) < half

    def split(x, axis):
        zero = jnp.zeros_like(x)
        return jnp.concatenate([jnp.where(left, x, zero), jnp.where(left, zero, x)], axis=axis)

    def factors(i):
        weight = tab[i, 2 * pad : 3 * pad, :]
        return [(tab[i, h * pad : (h + 1) * pad, :], weight) for h in range(2)]

    steps = ((0, 4), (2, 1), (6, 5), (3, 7))

    def gather_state(i):
        vt = vbuf[i].astype(jnp.float32).T
        vt_buf[i] = vt.astype(jnp.bfloat16)
        parts, fades = [], []
        for h, (cumul, weight) in enumerate(factors(i)):
            last = cumul[:, tok - 1 : tok]
            faded = jnp.where(weight > 0.0, jnp.exp(last - cumul), 0.0)
            mine = vt[h * half : (h + 1) * half, :]
            parts.append(
                jnp.concatenate([mine * faded[m : m + 1, :] for m in range(slots)], axis=0)
            )
            fades.append(jnp.broadcast_to(jnp.exp(last), (pad, 128)))
        scaled = jnp.concatenate(parts, axis=1).astype(jnp.bfloat16)
        t_buf[i] = mm(scaled, split(kbuf[i], 0))
        fade_buf[i] = jnp.where(left, fades[0], fades[1])

    for step in steps:
        for j in step:
            if j == 0:
                own[0].wait()
                own[1].wait()
            else:
                for kind in range(3):
                    transfer(kind, j).wait_recv()
        for j in step:
            gather_state(peers[j])

    for m in range(slots):
        rows = pl.ds(m * half, half)
        state = jnp.zeros((half, 128), jnp.float32)
        kept = jnp.ones((1, 128), jnp.float32)
        for i in range(GROUP):
            fade = fade_buf[i, m : m + 1, :]
            added = t_buf[i, rows, :]
            t_buf[i, rows, :] = state
            pre_buf[i, m : m + 1, :] = kept
            state = fade * state + added
            kept = kept * fade
        total_buf[group, rows, :] = state.astype(jnp.bfloat16)
        keep_buf[group, m : m + 1, :] = kept

    def exchange(j):
        to = device(other(j) * GROUP + rank)
        return [
            pltpu.make_async_remote_copy(
                src_ref=ref.at[group],
                dst_ref=ref.at[group],
                send_sem=tot_send.at[kind, j],
                recv_sem=tot_recv.at[kind, j],
                device_id=to,
                device_id_type=MESH,
            )
            for kind, ref in enumerate((total_buf, keep_buf))
        ]

    def launch_totals(j, _):
        for copy in exchange(j):
            copy.start()
        return 0

    lax.fori_loop(1, groups, launch_totals, 0)

    def inside(i):
        scores = mm(kbuf[i], split(qbuf[i], 0), NT)
        for h, (cumul, weight) in enumerate(factors(i)):
            middle = 0.5 * cumul[:, tok - 1 : tok]
            read_hi, read_lo = halves(weight * jnp.exp(cumul - middle))
            write_hi, write_lo = halves(jnp.where(weight > 0.0, jnp.exp(middle - cumul), 0.0))
            factor = mm(
                jnp.concatenate([write_hi, write_lo, write_hi], axis=0),
                jnp.concatenate([read_hi, read_hi, read_lo], axis=0),
                TN,
            )
            part = scores[:, h * tok : (h + 1) * tok] * factor
            part = jnp.where(causal, part, 0.0).astype(jnp.bfloat16)
            inner_buf[i, :, h * tok : (h + 1) * tok] = mm(
                vt_buf[i, h * half : (h + 1) * half, :], part
            )

    def arrive_and_inside(step):
        for j in step:
            if j == 0:
                own[2].wait()
            else:
                transfer(3, j).wait_recv()
        for j in step:
            inside(peers[j])

    back = ((2, 6), (3, 7), (1, 5), (4, 0))
    arrive_and_inside(back[0])

    def await_totals(j, _):
        for copy in exchange(j):
            copy.wait_recv()
        return 0

    lax.fori_loop(1, groups, await_totals, 0)

    def carry(g, state):
        parts = []
        for m in range(slots):
            before = state[m * half : (m + 1) * half, :]
            new = keep_buf[g, m : m + 1, :] * before + total_buf[
                g, m * half : (m + 1) * half, :
            ].astype(jnp.float32)
            parts.append(jnp.where(g < group, new, before))
        return jnp.concatenate(parts, axis=0)

    carried = lax.fori_loop(
        0, groups, carry, jnp.zeros((slots * half, 128), jnp.float32), unroll=groups <= 8
    )
    gain = gain_buf[rank]

    def give_back(j):
        return pltpu.make_async_remote_copy(
            src_ref=send_buf.at[peers[j]],
            dst_ref=columns(out_ref, rank),
            send_sem=out_send.at[j],
            recv_sem=out_recv.at[j],
            device_id=devices[j],
            device_id_type=MESH,
        )

    def finish(i):
        state = jnp.concatenate(
            [
                t_buf[i, m * half : (m + 1) * half, :]
                + pre_buf[i, m : m + 1, :] * carried[m * half : (m + 1) * half, :]
                for m in range(slots)
            ],
            axis=0,
        )
        read = mm(state.astype(jnp.bfloat16), split(qbuf[i], 0), NT)
        level = jnp.concatenate(
            [weight * jnp.exp(cumul) for cumul, weight in factors(i)], axis=1
        )
        total = inner_buf[i]
        for m in range(slots):
            total = total + level[m : m + 1, :] * read[m * half : (m + 1) * half, :]
        scale = lax.rsqrt(jnp.mean(total * total, axis=0, keepdims=True) + 1e-06)
        normed = total * scale
        flat = jnp.concatenate([normed[:, :tok], normed[:, tok:]], axis=0)
        send_buf[i] = (flat.T * gain).astype(jnp.bfloat16)

    for number, step in enumerate(back):
        if number > 0:
            arrive_and_inside(step)
        for j in step:
            finish(peers[j])
        for j in step:
            if j > 0:
                give_back(j).start()

    keep_own = pltpu.make_async_copy(
        send_buf.at[rank], columns(out_ref, rank), own_sem.at[3]
    )
    keep_own.start()

    for j in range(1, GROUP):
        for kind in range(4):
            transfer(kind, j).wait_send()
        copy = give_back(j)
        copy.wait_send()
        copy.wait_recv()

    def drain_totals(j, _):
        for copy in exchange(j):
            copy.wait_send()
        return 0

    lax.fori_loop(1, groups, drain_totals, 0)
    keep_own.wait()


def on_device(queries, key_vectors, value_vectors, log_decay, routes, route_weight, out_gain):
    n_ctx, n_mem = lax.axis_size("ctx"), lax.axis_size("mem")
    tok, width = queries.shape
    heads = log_decay.shape[1]
    groups = n_ctx * n_mem // GROUP
    slots = n_mem + 1
    pad = (slots + 7) // 8 * 8
    gain = out_gain.reshape(GROUP, 1, 128)
    hbm = pl.BlockSpec(memory_space=pltpu.HBM)
    return pl.pallas_call(
        functools.partial(kernel, n_ctx, n_mem, heads, pad),
        out_shape=jax.ShapeDtypeStruct((tok, width), jnp.bfloat16),
        in_specs=[hbm] * 7,
        out_specs=hbm,
        scratch_shapes=[
            pltpu.VMEM((GROUP, tok, 128), jnp.bfloat16),
            pltpu.VMEM((GROUP, tok, 128), jnp.bfloat16),
            pltpu.VMEM((GROUP, tok, 128), jnp.bfloat16),
            pltpu.VMEM((GROUP, 3 * pad, tok), jnp.float32),
            pltpu.VMEM((GROUP, 3 * pad, tok), jnp.float32),
            pltpu.VMEM((GROUP, 128, tok), jnp.bfloat16),
            pltpu.VMEM((GROUP, slots * 64, 128), jnp.float32),
            pltpu.VMEM((GROUP, pad, 128), jnp.float32),
            pltpu.VMEM((GROUP, pad, 128), jnp.float32),
            pltpu.VMEM((GROUP, 64, 2 * tok), jnp.float32),
            pltpu.VMEM((GROUP, tok, 128), jnp.bfloat16),
            pltpu.VMEM((groups, slots * 64, 128), jnp.bfloat16),
            pltpu.VMEM((groups, pad, 128), jnp.float32),
            pltpu.VMEM((heads, tok), jnp.bfloat16),
            pltpu.VMEM((2, tok), jnp.int32),
            pltpu.VMEM((2, tok), jnp.float32),
            pltpu.VMEM((GROUP, 1, 128), jnp.float32),
            pltpu.SemaphoreType.DMA((4, GROUP)),
            pltpu.SemaphoreType.DMA((4, GROUP)),
            pltpu.SemaphoreType.DMA((GROUP,)),
            pltpu.SemaphoreType.DMA((GROUP,)),
            pltpu.SemaphoreType.DMA((2, groups)),
            pltpu.SemaphoreType.DMA((2, groups)),
            pltpu.SemaphoreType.DMA((4,)),
            pltpu.SemaphoreType.DMA((4,)),
        ],
        compiler_params=pltpu.CompilerParams(
            collective_id=0, has_side_effects=True, vmem_limit_bytes=63 * 1024 * 1024
        ),
        cost_estimate=pl.CostEstimate(
            flops=2 * GROUP * 128 * 128 * 128 * 20, bytes_accessed=4 << 20, transcendentals=0
        ),
    )(queries, key_vectors, value_vectors, log_decay.T, routes.T, route_weight.T, gain)


def solution(mesh):
    rows = P(("ctx", "mem"), None)
    return jax.shard_map(
        on_device,
        mesh=mesh,
        in_specs=(rows, rows, rows, rows, rows, rows, P()),
        out_specs=rows,
        check_vma=False,
    )
```

```python
import functools

import jax
import jax.numpy as jnp
from jax import lax
from jax.experimental import pallas as pl
from jax.experimental.pallas import tpu as pltpu
from jax.sharding import PartitionSpec as P

MESH = pl.DeviceIdType.MESH
GROUP = 8
NT = (((1,), (1,)), ((), ()))
TN = (((0,), (0,)), ((), ()))


def mm(a, b, dims=(((1,), (0,)), ((), ()))):
    return lax.dot_general(a, b, dims, preferred_element_type=jnp.float32)


def halves(x):
    high = x.astype(jnp.bfloat16)
    return high, (x - high.astype(jnp.float32)).astype(jnp.bfloat16)


def kernel(
    n_ctx, n_mem, n_heads, pad,
    q_ref, k_ref, v_ref, decay_ref, routes_ref, weight_ref, gain_ref, out_ref,
    qbuf, kvbuf, q_mine, kv_mine, tab_mine, tab, vt_buf, t_buf, fade_buf, pre_buf, inner_buf, send_buf,
    total_buf, keep_buf, decay_buf, routes_buf, weight_buf, gain_buf,
    send_sem, recv_sem, out_send, out_recv, tot_send, tot_recv, own_sem, small_sem, stage_sem,
):
    slots = n_mem + 1
    groups = n_ctx * n_mem // GROUP
    tok = q_ref.shape[0]
    half = 64
    me = lax.axis_index("ctx") * n_mem + lax.axis_index("mem")
    group = lax.div(me, GROUP)
    rank = lax.rem(me, GROUP)

    def device(block):
        return (lax.div(block, n_mem), lax.rem(block, n_mem))

    def flipped(j):
        partner = rank
        for bit in (1, 2, 4):
            if j & bit:
                partner = partner + bit - 2 * bit * lax.rem(lax.div(rank, bit), 2)
        return partner

    peers = [flipped(j) for j in range(GROUP)]
    devices = [device(group * GROUP + r) for r in peers]

    def other(j):
        return lax.rem(group + j, groups)

    small = [
        pltpu.make_async_copy(src, dst, small_sem.at[i])
        for i, (src, dst) in enumerate(
            (
                (decay_ref, decay_buf),
                (routes_ref, routes_buf),
                (weight_ref, weight_buf),
                (gain_ref, gain_buf),
            )
        )
    ]
    for copy in small:
        copy.start()

    def columns(ref, r):
        return ref.at[:, pl.ds(pl.multiple_of(r * 128, 128), 128)]

    send_order = (4, 2, 1, 6, 5, 3, 7)
    back = ((2, 6), (3, 7), (1, 5), (4, 0))

    def stage(kind, j):
        src = columns((k_ref, v_ref, q_ref)[kind], peers[j])
        if kind == 2:
            dst = qbuf.at[rank] if j == 0 else q_mine.at[peers[j]]
        else:
            dst = kvbuf.at[rank, kind] if j == 0 else kv_mine.at[peers[j], kind]
        return pltpu.make_async_copy(src, dst, stage_sem.at[kind, j])

    for kinds in ((0, 1), (2,)):
        for j in send_order + (0,):
            for kind in kinds:
                stage(kind, j).start()

    barrier = pltpu.get_barrier_semaphore()
    for j in range(1, GROUP):
        pl.semaphore_signal(barrier, inc=1, device_id=devices[j], device_id_type=MESH)

    def greet_group(j, _):
        pl.semaphore_signal(
            barrier, inc=1, device_id=device(other(j) * GROUP + rank), device_id_type=MESH
        )
        return 0

    lax.fori_loop(1, groups, greet_group, 0)

    row = lax.broadcasted_iota(jnp.int32, (tok, tok), 0)
    col = lax.broadcasted_iota(jnp.int32, (tok, tok), 1)
    causal = row <= col
    upper = jnp.where(causal, 1.0, 0.0).astype(jnp.bfloat16)
    tab_mine[...] = jnp.zeros_like(tab_mine)
    for copy in small:
        copy.wait()
    decay = decay_buf[...].astype(jnp.float32)
    first, second = routes_buf[0:1, :], routes_buf[1:2, :]
    w_first, w_second = weight_buf[0:1, :], weight_buf[1:2, :]
    for m in range(slots):
        if m == 0:
            masked, weight = decay, jnp.ones_like(w_first)
        else:
            in_first, in_second = first == m - 1, second == m - 1
            masked = jnp.where(in_first | in_second, decay, 0.0)
            weight = jnp.where(in_first, w_first, jnp.where(in_second, w_second, 0.0))
        cumul = mm(masked.astype(jnp.bfloat16), upper)
        for p in range(GROUP):
            for h in range(2):
                tab_mine[p, h * pad + m : h * pad + m + 1, :] = cumul[2 * p + h : 2 * p + h + 1, :]
            tab_mine[p, 2 * pad + m : 2 * pad + m + 1, :] = weight

    pl.semaphore_wait(barrier, GROUP - 1 + groups - 1)

    def transfer(kind, j):
        to = peers[j]
        src, dst = (
            (tab_mine.at[to], tab.at[rank]),
            (kv_mine.at[to], kvbuf.at[rank]),
            (q_mine.at[to], qbuf.at[rank]),
        )[kind]
        return pltpu.make_async_remote_copy(
            src_ref=src,
            dst_ref=dst,
            send_sem=send_sem.at[kind, j],
            recv_sem=recv_sem.at[kind, j],
            device_id=devices[j],
            device_id_type=MESH,
        )

    for j in send_order:
        transfer(0, j).start()
        for kind in range(2):
            stage(kind, j).wait()
        transfer(1, j).start()
    for step in back:
        for j in step:
            if j > 0:
                stage(2, j).wait()
                transfer(2, j).start()

    tab[rank] = tab_mine[rank]

    left = lax.broadcasted_iota(jnp.int32, (1, 128), 1) < half

    def split(x, axis):
        zero = jnp.zeros_like(x)
        return jnp.concatenate([jnp.where(left, x, zero), jnp.where(left, zero, x)], axis=axis)

    def factors(i):
        weight = tab[i, 2 * pad : 3 * pad, :]
        return [(tab[i, h * pad : (h + 1) * pad, :], weight) for h in range(2)]

    steps = ((0, 4), (2, 1), (6, 5), (3, 7))

    def gather_state(i):
        vt = kvbuf[i, 1].astype(jnp.float32).T
        vt_buf[i] = vt.astype(jnp.bfloat16)
        parts, fades = [], []
        for h, (cumul, weight) in enumerate(factors(i)):
            last = cumul[:, tok - 1 : tok]
            faded = jnp.where(weight > 0.0, jnp.exp(last - cumul), 0.0)
            mine = vt[h * half : (h + 1) * half, :]
            parts.append(
                jnp.concatenate([mine * faded[m : m + 1, :] for m in range(slots)], axis=0)
            )
            fades.append(jnp.broadcast_to(jnp.exp(last), (pad, 128)))
        scaled = jnp.concatenate(parts, axis=1).astype(jnp.bfloat16)
        t_buf[i] = mm(scaled, split(kvbuf[i, 0], 0))
        fade_buf[i] = jnp.where(left, fades[0], fades[1])

    for step in steps:
        for j in step:
            if j == 0:
                for kind in range(2):
                    stage(kind, 0).wait()
            else:
                for kind in range(2):
                    transfer(kind, j).wait_recv()
        for j in step:
            gather_state(peers[j])

    for m in range(slots):
        rows = pl.ds(m * half, half)
        state = jnp.zeros((half, 128), jnp.float32)
        kept = jnp.ones((1, 128), jnp.float32)
        for i in range(GROUP):
            fade = fade_buf[i, m : m + 1, :]
            added = t_buf[i, rows, :]
            t_buf[i, rows, :] = state
            pre_buf[i, m : m + 1, :] = kept
            state = fade * state + added
            kept = kept * fade
        total_buf[group, rows, :] = state.astype(jnp.bfloat16)
        keep_buf[group, m : m + 1, :] = kept

    def exchange(j):
        to = device(other(j) * GROUP + rank)
        return [
            pltpu.make_async_remote_copy(
                src_ref=ref.at[group],
                dst_ref=ref.at[group],
                send_sem=tot_send.at[kind, j],
                recv_sem=tot_recv.at[kind, j],
                device_id=to,
                device_id_type=MESH,
            )
            for kind, ref in enumerate((total_buf, keep_buf))
        ]

    def launch_totals(j, _):
        for copy in exchange(j):
            copy.start()
        return 0

    lax.fori_loop(1, groups, launch_totals, 0)

    def inside(i):
        scores = mm(kvbuf[i, 0], split(qbuf[i], 0), NT)
        for h, (cumul, weight) in enumerate(factors(i)):
            middle = 0.5 * cumul[:, tok - 1 : tok]
            read_hi, read_lo = halves(weight * jnp.exp(cumul - middle))
            write_hi, write_lo = halves(jnp.where(weight > 0.0, jnp.exp(middle - cumul), 0.0))
            factor = mm(
                jnp.concatenate([write_hi, write_lo, write_hi], axis=0),
                jnp.concatenate([read_hi, read_hi, read_lo], axis=0),
                TN,
            )
            part = scores[:, h * tok : (h + 1) * tok] * factor
            part = jnp.where(causal, part, 0.0).astype(jnp.bfloat16)
            inner_buf[i, :, h * tok : (h + 1) * tok] = mm(
                vt_buf[i, h * half : (h + 1) * half, :], part
            )

    def arrive_and_inside(step):
        for j in step:
            if j == 0:
                stage(2, 0).wait()
            else:
                transfer(2, j).wait_recv()
        for j in step:
            inside(peers[j])

    arrive_and_inside(back[0])

    def await_totals(j, _):
        for copy in exchange(j):
            copy.wait_recv()
        return 0

    lax.fori_loop(1, groups, await_totals, 0)

    def carry(g, state):
        parts = []
        for m in range(slots):
            before = state[m * half : (m + 1) * half, :]
            new = keep_buf[g, m : m + 1, :] * before + total_buf[
                g, m * half : (m + 1) * half, :
            ].astype(jnp.float32)
            parts.append(jnp.where(g < group, new, before))
        return jnp.concatenate(parts, axis=0)

    carried = lax.fori_loop(
        0, groups, carry, jnp.zeros((slots * half, 128), jnp.float32), unroll=groups <= 8
    )
    gain = gain_buf[rank]

    def give_back(j):
        return pltpu.make_async_remote_copy(
            src_ref=send_buf.at[peers[j]],
            dst_ref=columns(out_ref, rank),
            send_sem=out_send.at[j],
            recv_sem=out_recv.at[j],
            device_id=devices[j],
            device_id_type=MESH,
        )

    def finish(i):
        state = jnp.concatenate(
            [
                t_buf[i, m * half : (m + 1) * half, :]
                + pre_buf[i, m : m + 1, :] * carried[m * half : (m + 1) * half, :]
                for m in range(slots)
            ],
            axis=0,
        )
        read = mm(state.astype(jnp.bfloat16), split(qbuf[i], 0), NT)
        level = jnp.concatenate(
            [weight * jnp.exp(cumul) for cumul, weight in factors(i)], axis=1
        )
        total = inner_buf[i]
        for m in range(slots):
            total = total + level[m : m + 1, :] * read[m * half : (m + 1) * half, :]
        scale = lax.rsqrt(jnp.mean(total * total, axis=0, keepdims=True) + 1e-06)
        normed = total * scale
        flat = jnp.concatenate([normed[:, :tok], normed[:, tok:]], axis=0)
        send_buf[i] = (flat.T * gain).astype(jnp.bfloat16)

    for number, step in enumerate(back):
        if number > 0:
            arrive_and_inside(step)
        for j in step:
            finish(peers[j])
        for j in step:
            if j > 0:
                give_back(j).start()

    keep_own = pltpu.make_async_copy(
        send_buf.at[rank], columns(out_ref, rank), own_sem.at[0]
    )
    keep_own.start()

    for j in range(1, GROUP):
        for kind in range(3):
            transfer(kind, j).wait_send()
        copy = give_back(j)
        copy.wait_send()
        copy.wait_recv()

    def drain_totals(j, _):
        for copy in exchange(j):
            copy.wait_send()
        return 0

    lax.fori_loop(1, groups, drain_totals, 0)
    keep_own.wait()


def on_device(queries, key_vectors, value_vectors, log_decay, routes, route_weight, out_gain):
    n_ctx, n_mem = lax.axis_size("ctx"), lax.axis_size("mem")
    tok, width = queries.shape
    heads = log_decay.shape[1]
    groups = n_ctx * n_mem // GROUP
    slots = n_mem + 1
    pad = (slots + 7) // 8 * 8
    gain = out_gain.reshape(GROUP, 1, 128)
    hbm = pl.BlockSpec(memory_space=pltpu.HBM)
    return pl.pallas_call(
        functools.partial(kernel, n_ctx, n_mem, heads, pad),
        out_shape=jax.ShapeDtypeStruct((tok, width), jnp.bfloat16),
        in_specs=[hbm] * 7,
        out_specs=hbm,
        scratch_shapes=[
            pltpu.VMEM((GROUP, tok, 128), jnp.bfloat16),
            pltpu.VMEM((GROUP, 2, tok, 128), jnp.bfloat16),
            pltpu.VMEM((GROUP, tok, 128), jnp.bfloat16),
            pltpu.VMEM((GROUP, 2, tok, 128), jnp.bfloat16),
            pltpu.VMEM((GROUP, 3 * pad, tok), jnp.float32),
            pltpu.VMEM((GROUP, 3 * pad, tok), jnp.float32),
            pltpu.VMEM((GROUP, 128, tok), jnp.bfloat16),
            pltpu.VMEM((GROUP, slots * 64, 128), jnp.float32),
            pltpu.VMEM((GROUP, pad, 128), jnp.float32),
            pltpu.VMEM((GROUP, pad, 128), jnp.float32),
            pltpu.VMEM((GROUP, 64, 2 * tok), jnp.float32),
            pltpu.VMEM((GROUP, tok, 128), jnp.bfloat16),
            pltpu.VMEM((groups, slots * 64, 128), jnp.bfloat16),
            pltpu.VMEM((groups, pad, 128), jnp.float32),
            pltpu.VMEM((heads, tok), jnp.bfloat16),
            pltpu.VMEM((2, tok), jnp.int32),
            pltpu.VMEM((2, tok), jnp.float32),
            pltpu.VMEM((GROUP, 1, 128), jnp.float32),
            pltpu.SemaphoreType.DMA((3, GROUP)),
            pltpu.SemaphoreType.DMA((3, GROUP)),
            pltpu.SemaphoreType.DMA((GROUP,)),
            pltpu.SemaphoreType.DMA((GROUP,)),
            pltpu.SemaphoreType.DMA((2, groups)),
            pltpu.SemaphoreType.DMA((2, groups)),
            pltpu.SemaphoreType.DMA((1,)),
            pltpu.SemaphoreType.DMA((4,)),
            pltpu.SemaphoreType.DMA((3, GROUP)),
        ],
        compiler_params=pltpu.CompilerParams(
            collective_id=0, has_side_effects=True, vmem_limit_bytes=63 * 1024 * 1024
        ),
        cost_estimate=pl.CostEstimate(
            flops=2 * GROUP * 128 * 128 * 128 * 20, bytes_accessed=4 << 20, transcendentals=0
        ),
    )(queries, key_vectors, value_vectors, log_decay.T, routes.T, route_weight.T, gain)


def solution(mesh):
    rows = P(("ctx", "mem"), None)
    return jax.shard_map(
        on_device,
        mesh=mesh,
        in_specs=(rows, rows, rows, rows, rows, rows, P()),
        out_specs=rows,
        check_vma=False,
    )
```

```python
import functools

import jax
import jax.numpy as jnp
from jax import lax
from jax.experimental import pallas as pl
from jax.experimental.pallas import tpu as pltpu
from jax.sharding import PartitionSpec as P

MESH = pl.DeviceIdType.MESH
GROUP = 8
NT = (((1,), (1,)), ((), ()))
TN = (((0,), (0,)), ((), ()))


def mm(a, b, dims=(((1,), (0,)), ((), ()))):
    return lax.dot_general(a, b, dims, preferred_element_type=jnp.float32)


def halves(x):
    high = x.astype(jnp.bfloat16)
    return high, (x - high.astype(jnp.float32)).astype(jnp.bfloat16)


def kernel(
    n_ctx, n_mem, n_heads, pad,
    q_ref, k_ref, v_ref, decay_ref, routes_ref, weight_ref, gain_ref, out_ref,
    qbuf, kvbuf, q_mine, kv_mine, tab_mine, tab, cum_buf, vt_buf, t_buf, fade_buf, pre_buf, inner_buf, send_buf,
    total_buf, keep_buf, decay_buf, routes_buf, weight_buf, gain_buf,
    send_sem, recv_sem, out_send, out_recv, tot_send, tot_recv, own_sem, small_sem, stage_sem,
):
    slots = n_mem + 1
    groups = n_ctx * n_mem // GROUP
    tok = q_ref.shape[0]
    half = 64
    me = lax.axis_index("ctx") * n_mem + lax.axis_index("mem")
    group = lax.div(me, GROUP)
    rank = lax.rem(me, GROUP)

    def device(block):
        return (lax.div(block, n_mem), lax.rem(block, n_mem))

    def flipped(j):
        partner = rank
        for bit in (1, 2, 4):
            if j & bit:
                partner = partner + bit - 2 * bit * lax.rem(lax.div(rank, bit), 2)
        return partner

    peers = [flipped(j) for j in range(GROUP)]
    devices = [device(group * GROUP + r) for r in peers]

    def other(j):
        return lax.rem(group + j, groups)

    small = [
        pltpu.make_async_copy(src, dst, small_sem.at[i])
        for i, (src, dst) in enumerate(
            (
                (decay_ref, decay_buf),
                (routes_ref, routes_buf),
                (weight_ref, weight_buf),
                (gain_ref, gain_buf),
            )
        )
    ]
    for copy in small:
        copy.start()

    def columns(ref, r):
        return ref.at[:, pl.ds(pl.multiple_of(r * 128, 128), 128)]

    send_order = (4, 2, 1, 6, 5, 3, 7)
    back = ((2, 6), (3, 7), (1, 5), (4, 0))

    def stage(kind, j):
        src = columns((k_ref, v_ref, q_ref)[kind], peers[j])
        if kind == 2:
            dst = qbuf.at[rank] if j == 0 else q_mine.at[peers[j]]
        else:
            dst = kvbuf.at[rank, kind] if j == 0 else kv_mine.at[peers[j], kind]
        return pltpu.make_async_copy(src, dst, stage_sem.at[kind, j])

    for kinds in ((0, 1), (2,)):
        for j in send_order + (0,):
            for kind in kinds:
                stage(kind, j).start()

    barrier = pltpu.get_barrier_semaphore()
    for j in range(1, GROUP):
        pl.semaphore_signal(barrier, inc=1, device_id=devices[j], device_id_type=MESH)

    def greet_group(j, _):
        pl.semaphore_signal(
            barrier, inc=1, device_id=device(other(j) * GROUP + rank), device_id_type=MESH
        )
        return 0

    lax.fori_loop(1, groups, greet_group, 0)

    row = lax.broadcasted_iota(jnp.int32, (tok, tok), 0)
    col = lax.broadcasted_iota(jnp.int32, (tok, tok), 1)
    causal = row <= col
    upper = jnp.where(causal, 1.0, 0.0).astype(jnp.bfloat16)
    for copy in small:
        copy.wait()
    decay = decay_buf[...].astype(jnp.float32)
    first, second = routes_buf[0:1, :], routes_buf[1:2, :]
    w_first, w_second = weight_buf[0:1, :], weight_buf[1:2, :]
    weights = [jnp.ones_like(w_first)] + [
        jnp.where(first == m, w_first, jnp.where(second == m, w_second, 0.0))
        for m in range(n_mem)
    ]
    tab_mine[...] = jnp.zeros_like(tab_mine)
    for p in range(GROUP):
        for m in range(slots):
            tab_mine[p, m : m + 1, :] = weights[m]
        tab_mine[p, slots : slots + 2, :] = decay[2 * p : 2 * p + 2, :]

    pl.semaphore_wait(barrier, GROUP - 1 + groups - 1)

    def transfer(kind, j):
        to = peers[j]
        src, dst = (
            (tab_mine.at[to], tab.at[rank]),
            (kv_mine.at[to], kvbuf.at[rank]),
            (q_mine.at[to], qbuf.at[rank]),
        )[kind]
        return pltpu.make_async_remote_copy(
            src_ref=src,
            dst_ref=dst,
            send_sem=send_sem.at[kind, j],
            recv_sem=recv_sem.at[kind, j],
            device_id=devices[j],
            device_id_type=MESH,
        )

    for j in send_order:
        transfer(0, j).start()
        for kind in range(2):
            stage(kind, j).wait()
        transfer(1, j).start()
    for step in back:
        for j in step:
            if j > 0:
                stage(2, j).wait()
                transfer(2, j).start()

    tab[rank] = tab_mine[rank]

    left = lax.broadcasted_iota(jnp.int32, (1, 128), 1) < half

    def split(x, axis):
        zero = jnp.zeros_like(x)
        return jnp.concatenate([jnp.where(left, x, zero), jnp.where(left, zero, x)], axis=axis)

    def factors(i):
        weight = tab[i]
        return [(cum_buf[i, h * pad : (h + 1) * pad, :], weight) for h in range(2)]

    steps = ((0, 4), (2, 1), (6, 5), (3, 7))

    def gather_state(i):
        member = tab[i] > 0.0
        masked = [
            jnp.where(member, tab[i, slots + h : slots + h + 1, :], 0.0) for h in range(2)
        ]
        cum_buf[i] = mm(jnp.concatenate(masked, axis=0).astype(jnp.bfloat16), upper)
        vt = kvbuf[i, 1].astype(jnp.float32).T
        vt_buf[i] = vt.astype(jnp.bfloat16)
        parts, fades = [], []
        for h, (cumul, weight) in enumerate(factors(i)):
            last = cumul[:, tok - 1 : tok]
            faded = jnp.where(weight > 0.0, jnp.exp(last - cumul), 0.0)
            mine = vt[h * half : (h + 1) * half, :]
            parts.append(
                jnp.concatenate([mine * faded[m : m + 1, :] for m in range(slots)], axis=0)
            )
            fades.append(jnp.broadcast_to(jnp.exp(last), (pad, 128)))
        scaled = jnp.concatenate(parts, axis=1).astype(jnp.bfloat16)
        t_buf[i] = mm(scaled, split(kvbuf[i, 0], 0))
        fade_buf[i] = jnp.where(left, fades[0], fades[1])

    for step in steps:
        for j in step:
            if j == 0:
                for kind in range(2):
                    stage(kind, 0).wait()
            else:
                for kind in range(2):
                    transfer(kind, j).wait_recv()
        for j in step:
            gather_state(peers[j])

    def exchange(j, part):
        if part == slots:
            mine = keep_buf.at[group]
        else:
            mine = total_buf.at[group, pl.ds(part * half, half)]
        return pltpu.make_async_remote_copy(
            src_ref=mine,
            dst_ref=mine,
            send_sem=tot_send.at[part, j],
            recv_sem=tot_recv.at[part, j],
            device_id=device(other(j) * GROUP + rank),
            device_id_type=MESH,
        )

    def each_group(part, act):
        def run(j, _):
            act(exchange(j, part))
            return 0

        lax.fori_loop(1, groups, run, 0)

    kept = jnp.ones((pad, 128), jnp.float32)
    for i in range(GROUP):
        pre_buf[i] = kept
        kept = kept * fade_buf[i]
    keep_buf[group] = kept
    each_group(slots, lambda copy: copy.start())
    for m in range(slots):
        rows = pl.ds(m * half, half)
        state = t_buf[0, rows, :]
        t_buf[0, rows, :] = jnp.zeros((half, 128), jnp.float32)
        for i in range(1, GROUP):
            added = t_buf[i, rows, :]
            t_buf[i, rows, :] = state
            state = fade_buf[i, m : m + 1, :] * state + added
        total_buf[group, rows, :] = state.astype(jnp.bfloat16)
        each_group(m, lambda copy: copy.start())

    def inside(i):
        scores = mm(kvbuf[i, 0], split(qbuf[i], 0), NT)
        for h, (cumul, weight) in enumerate(factors(i)):
            middle = 0.5 * cumul[:, tok - 1 : tok]
            read_hi, read_lo = halves(weight * jnp.exp(cumul - middle))
            write_hi, write_lo = halves(jnp.where(weight > 0.0, jnp.exp(middle - cumul), 0.0))
            factor = mm(
                jnp.concatenate([write_hi, write_lo, write_hi], axis=0),
                jnp.concatenate([read_hi, read_hi, read_lo], axis=0),
                TN,
            )
            part = scores[:, h * tok : (h + 1) * tok] * factor
            part = jnp.where(causal, part, 0.0).astype(jnp.bfloat16)
            inner_buf[i, :, h * tok : (h + 1) * tok] = mm(
                vt_buf[i, h * half : (h + 1) * half, :], part
            )

    def arrive_and_inside(step):
        for j in step:
            if j == 0:
                stage(2, 0).wait()
            else:
                transfer(2, j).wait_recv()
        for j in step:
            inside(peers[j])

    arrive_and_inside(back[0])

    each_group(slots, lambda copy: copy.wait_recv())
    carried = []
    for m in range(slots):
        each_group(m, lambda copy: copy.wait_recv())

        def carry(g, before, m=m):
            added = total_buf[g, m * half : (m + 1) * half, :].astype(jnp.float32)
            new = keep_buf[g, m : m + 1, :] * before + added
            return jnp.where(g < group, new, before)

        carried.append(
            lax.fori_loop(
                0, groups, carry, jnp.zeros((half, 128), jnp.float32), unroll=groups <= 8
            )
        )
    gain = gain_buf[rank]

    def give_back(j):
        return pltpu.make_async_remote_copy(
            src_ref=send_buf.at[peers[j]],
            dst_ref=columns(out_ref, rank),
            send_sem=out_send.at[j],
            recv_sem=out_recv.at[j],
            device_id=devices[j],
            device_id_type=MESH,
        )

    def finish(i):
        state = jnp.concatenate(
            [
                t_buf[i, m * half : (m + 1) * half, :]
                + pre_buf[i, m : m + 1, :] * carried[m]
                for m in range(slots)
            ],
            axis=0,
        )
        read = mm(state.astype(jnp.bfloat16), split(qbuf[i], 0), NT)
        level = jnp.concatenate(
            [weight * jnp.exp(cumul) for cumul, weight in factors(i)], axis=1
        )
        total = inner_buf[i]
        for m in range(slots):
            total = total + level[m : m + 1, :] * read[m * half : (m + 1) * half, :]
        scale = lax.rsqrt(jnp.mean(total * total, axis=0, keepdims=True) + 1e-06)
        normed = total * scale
        flat = jnp.concatenate([normed[:, :tok], normed[:, tok:]], axis=0)
        send_buf[i] = (flat.T * gain).astype(jnp.bfloat16)

    for number, step in enumerate(back):
        if number > 0:
            arrive_and_inside(step)
        for j in step:
            finish(peers[j])
        for j in step:
            if j > 0:
                give_back(j).start()

    keep_own = pltpu.make_async_copy(
        send_buf.at[rank], columns(out_ref, rank), own_sem.at[0]
    )
    keep_own.start()

    for j in range(1, GROUP):
        for kind in range(3):
            transfer(kind, j).wait_send()
        copy = give_back(j)
        copy.wait_send()
        copy.wait_recv()

    for part in range(slots + 1):
        each_group(part, lambda copy: copy.wait_send())
    keep_own.wait()


def on_device(queries, key_vectors, value_vectors, log_decay, routes, route_weight, out_gain):
    n_ctx, n_mem = lax.axis_size("ctx"), lax.axis_size("mem")
    tok, width = queries.shape
    heads = log_decay.shape[1]
    groups = n_ctx * n_mem // GROUP
    slots = n_mem + 1
    pad = (slots + 9) // 8 * 8
    gain = out_gain.reshape(GROUP, 1, 128)
    hbm = pl.BlockSpec(memory_space=pltpu.HBM)
    return pl.pallas_call(
        functools.partial(kernel, n_ctx, n_mem, heads, pad),
        out_shape=jax.ShapeDtypeStruct((tok, width), jnp.bfloat16),
        in_specs=[hbm] * 7,
        out_specs=hbm,
        scratch_shapes=[
            pltpu.VMEM((GROUP, tok, 128), jnp.bfloat16),
            pltpu.VMEM((GROUP, 2, tok, 128), jnp.bfloat16),
            pltpu.VMEM((GROUP, tok, 128), jnp.bfloat16),
            pltpu.VMEM((GROUP, 2, tok, 128), jnp.bfloat16),
            pltpu.VMEM((GROUP, pad, tok), jnp.float32),
            pltpu.VMEM((GROUP, pad, tok), jnp.float32),
            pltpu.VMEM((GROUP, 2 * pad, tok), jnp.float32),
            pltpu.VMEM((GROUP, 128, tok), jnp.bfloat16),
            pltpu.VMEM((GROUP, slots * 64, 128), jnp.float32),
            pltpu.VMEM((GROUP, pad, 128), jnp.float32),
            pltpu.VMEM((GROUP, pad, 128), jnp.float32),
            pltpu.VMEM((GROUP, 64, 2 * tok), jnp.float32),
            pltpu.VMEM((GROUP, tok, 128), jnp.bfloat16),
            pltpu.VMEM((groups, slots * 64, 128), jnp.bfloat16),
            pltpu.VMEM((groups, pad, 128), jnp.float32),
            pltpu.VMEM((heads, tok), jnp.bfloat16),
            pltpu.VMEM((2, tok), jnp.int32),
            pltpu.VMEM((2, tok), jnp.float32),
            pltpu.VMEM((GROUP, 1, 128), jnp.float32),
            pltpu.SemaphoreType.DMA((3, GROUP)),
            pltpu.SemaphoreType.DMA((3, GROUP)),
            pltpu.SemaphoreType.DMA((GROUP,)),
            pltpu.SemaphoreType.DMA((GROUP,)),
            pltpu.SemaphoreType.DMA((slots + 1, groups)),
            pltpu.SemaphoreType.DMA((slots + 1, groups)),
            pltpu.SemaphoreType.DMA((1,)),
            pltpu.SemaphoreType.DMA((4,)),
            pltpu.SemaphoreType.DMA((3, GROUP)),
        ],
        compiler_params=pltpu.CompilerParams(
            collective_id=0, has_side_effects=True, vmem_limit_bytes=63 * 1024 * 1024
        ),
        cost_estimate=pl.CostEstimate(
            flops=2 * GROUP * 128 * 128 * 128 * 20, bytes_accessed=4 << 20, transcendentals=0
        ),
    )(queries, key_vectors, value_vectors, log_decay.T, routes.T, route_weight.T, gain)


def solution(mesh):
    rows = P(("ctx", "mem"), None)
    return jax.shard_map(
        on_device,
        mesh=mesh,
        in_specs=(rows, rows, rows, rows, rows, rows, P()),
        out_specs=rows,
        check_vma=False,
    )
```

```python
import functools

import jax
import jax.numpy as jnp
from jax import lax
from jax.experimental import pallas as pl
from jax.experimental.pallas import tpu as pltpu
from jax.sharding import PartitionSpec as P

MESH = pl.DeviceIdType.MESH
GROUP = 8
NT = (((1,), (1,)), ((), ()))
TN = (((0,), (0,)), ((), ()))


def mm(a, b, dims=(((1,), (0,)), ((), ()))):
    return lax.dot_general(a, b, dims, preferred_element_type=jnp.float32)


def halves(x):
    high = x.astype(jnp.bfloat16)
    return high, (x - high.astype(jnp.float32)).astype(jnp.bfloat16)


def kernel(
    n_ctx, n_mem, n_heads, pad,
    q_ref, k_ref, v_ref, decay_ref, routes_ref, weight_ref, gain_ref, out_ref,
    qbuf, kvbuf, q_mine, kv_mine, tab_mine, tab, cum_buf, vt_buf, t_buf, fade_buf, pre_buf, inner_buf, send_buf,
    total_buf, keep_buf, decay_buf, routes_buf, weight_buf, gain_buf,
    send_sem, recv_sem, out_send, out_recv, tot_send, tot_recv, own_sem, small_sem, stage_sem,
):
    slots = n_mem + 1
    groups = n_ctx * n_mem // GROUP
    tok = q_ref.shape[0]
    half = 64
    me = lax.axis_index("ctx") * n_mem + lax.axis_index("mem")
    group = lax.div(me, GROUP)
    rank = lax.rem(me, GROUP)

    def device(block):
        return (lax.div(block, n_mem), lax.rem(block, n_mem))

    def flipped(j):
        partner = rank
        for bit in (1, 2, 4):
            if j & bit:
                partner = partner + bit - 2 * bit * lax.rem(lax.div(rank, bit), 2)
        return partner

    peers = [flipped(j) for j in range(GROUP)]
    devices = [device(group * GROUP + r) for r in peers]

    def other(j):
        return lax.rem(group + j, groups)

    barrier = pltpu.get_barrier_semaphore()
    for j in range(1, GROUP):
        pl.semaphore_signal(barrier, inc=1, device_id=devices[j], device_id_type=MESH)

    def greet_group(j, _):
        pl.semaphore_signal(
            barrier, inc=1, device_id=device(other(j) * GROUP + rank), device_id_type=MESH
        )
        return 0

    lax.fori_loop(1, groups, greet_group, 0)

    small = [
        pltpu.make_async_copy(src, dst, small_sem.at[i])
        for i, (src, dst) in enumerate(
            (
                (decay_ref, decay_buf),
                (routes_ref, routes_buf),
                (weight_ref, weight_buf),
                (gain_ref, gain_buf),
            )
        )
    ]
    for copy in small:
        copy.start()

    def columns(ref, r):
        return ref.at[:, pl.ds(pl.multiple_of(r * 128, 128), 128)]

    send_order = (4, 2, 1, 6, 5, 3, 7)
    back = ((2, 6), (3, 7), (1, 5), (4, 0))

    def stage(kind, j):
        src = columns((k_ref, v_ref, q_ref)[kind], peers[j])
        if kind == 2:
            dst = qbuf.at[rank] if j == 0 else q_mine.at[peers[j]]
        else:
            dst = kvbuf.at[rank, kind] if j == 0 else kv_mine.at[peers[j], kind]
        return pltpu.make_async_copy(src, dst, stage_sem.at[kind, j])

    for j in send_order + (0,):
        for kind in range(2):
            stage(kind, j).start()

    row = lax.broadcasted_iota(jnp.int32, (tok, tok), 0)
    col = lax.broadcasted_iota(jnp.int32, (tok, tok), 1)
    causal = row <= col
    upper = jnp.where(causal, 1.0, 0.0).astype(jnp.bfloat16)
    for copy in small:
        copy.wait()
    decay = decay_buf[...].astype(jnp.float32)
    first, second = routes_buf[0:1, :], routes_buf[1:2, :]
    w_first, w_second = weight_buf[0:1, :], weight_buf[1:2, :]
    weights = [jnp.ones_like(w_first)] + [
        jnp.where(first == m, w_first, jnp.where(second == m, w_second, 0.0))
        for m in range(n_mem)
    ]
    tab_mine[...] = jnp.zeros_like(tab_mine)
    for p in range(GROUP):
        for m in range(slots):
            tab_mine[p, m : m + 1, :] = weights[m]
        tab_mine[p, slots : slots + 2, :] = decay[2 * p : 2 * p + 2, :]

    pl.semaphore_wait(barrier, GROUP - 1 + groups - 1)

    def transfer(kind, j):
        to = peers[j]
        src, dst = (
            (tab_mine.at[to], tab.at[rank]),
            (kv_mine.at[to], kvbuf.at[rank]),
            (q_mine.at[to], qbuf.at[rank]),
        )[kind]
        return pltpu.make_async_remote_copy(
            src_ref=src,
            dst_ref=dst,
            send_sem=send_sem.at[kind, j],
            recv_sem=recv_sem.at[kind, j],
            device_id=devices[j],
            device_id_type=MESH,
        )

    for j in send_order:
        transfer(0, j).start()
        for kind in range(2):
            stage(kind, j).wait()
        transfer(1, j).start()
    for step in back:
        for j in step:
            stage(2, j).start()
    for step in back:
        for j in step:
            if j > 0:
                stage(2, j).wait()
                transfer(2, j).start()

    tab[rank] = tab_mine[rank]

    left = lax.broadcasted_iota(jnp.int32, (1, 128), 1) < half

    def split(x, axis):
        zero = jnp.zeros_like(x)
        return jnp.concatenate([jnp.where(left, x, zero), jnp.where(left, zero, x)], axis=axis)

    def factors(i):
        weight = tab[i]
        return [(cum_buf[i, h * pad : (h + 1) * pad, :], weight) for h in range(2)]

    steps = ((0, 4), (2, 1), (6, 5), (3, 7))

    def gather_state(i):
        member = tab[i] > 0.0
        masked = [
            jnp.where(member, tab[i, slots + h : slots + h + 1, :], 0.0) for h in range(2)
        ]
        cum_buf[i] = mm(jnp.concatenate(masked, axis=0).astype(jnp.bfloat16), upper)
        vt = kvbuf[i, 1].astype(jnp.float32).T
        vt_buf[i] = vt.astype(jnp.bfloat16)
        parts, fades = [], []
        for h, (cumul, weight) in enumerate(factors(i)):
            last = cumul[:, tok - 1 : tok]
            faded = jnp.where(weight > 0.0, jnp.exp(last - cumul), 0.0)
            mine = vt[h * half : (h + 1) * half, :]
            parts.append(
                jnp.concatenate([mine * faded[m : m + 1, :] for m in range(slots)], axis=0)
            )
            fades.append(jnp.broadcast_to(jnp.exp(last), (pad, 128)))
        scaled = jnp.concatenate(parts, axis=1).astype(jnp.bfloat16)
        t_buf[i] = mm(scaled, split(kvbuf[i, 0], 0))
        fade_buf[i] = jnp.where(left, fades[0], fades[1])

    for step in steps:
        for j in step:
            if j == 0:
                for kind in range(2):
                    stage(kind, 0).wait()
            else:
                for kind in range(2):
                    transfer(kind, j).wait_recv()
        for j in step:
            gather_state(peers[j])

    def exchange(j, part):
        if part == slots:
            mine = keep_buf.at[group]
        else:
            mine = total_buf.at[group, pl.ds(part * half, half)]
        return pltpu.make_async_remote_copy(
            src_ref=mine,
            dst_ref=mine,
            send_sem=tot_send.at[part, j],
            recv_sem=tot_recv.at[part, j],
            device_id=device(other(j) * GROUP + rank),
            device_id_type=MESH,
        )

    def each_group(part, act):
        def run(j, _):
            act(exchange(j, part))
            return 0

        lax.fori_loop(1, groups, run, 0)

    kept = jnp.ones((pad, 128), jnp.float32)
    for i in range(GROUP):
        pre_buf[i] = kept
        kept = kept * fade_buf[i]
    keep_buf[group] = kept
    each_group(slots, lambda copy: copy.start())
    for m in range(slots):
        rows = pl.ds(m * half, half)
        state = t_buf[0, rows, :]
        t_buf[0, rows, :] = jnp.zeros((half, 128), jnp.float32)
        for i in range(1, GROUP):
            added = t_buf[i, rows, :]
            t_buf[i, rows, :] = state
            state = fade_buf[i, m : m + 1, :] * state + added
        total_buf[group, rows, :] = state.astype(jnp.bfloat16)
        each_group(m, lambda copy: copy.start())

    def inside(i):
        scores = mm(kvbuf[i, 0], split(qbuf[i], 0), NT)
        for h, (cumul, weight) in enumerate(factors(i)):
            middle = 0.5 * cumul[:, tok - 1 : tok]
            read_hi, read_lo = halves(weight * jnp.exp(cumul - middle))
            write_hi, write_lo = halves(jnp.where(weight > 0.0, jnp.exp(middle - cumul), 0.0))
            factor = mm(
                jnp.concatenate([write_hi, write_lo, write_hi], axis=0),
                jnp.concatenate([read_hi, read_hi, read_lo], axis=0),
                TN,
            )
            part = scores[:, h * tok : (h + 1) * tok] * factor
            part = jnp.where(causal, part, 0.0).astype(jnp.bfloat16)
            inner_buf[i, :, h * tok : (h + 1) * tok] = mm(
                vt_buf[i, h * half : (h + 1) * half, :], part
            )

    def arrive_and_inside(step):
        for j in step:
            if j == 0:
                stage(2, 0).wait()
            else:
                transfer(2, j).wait_recv()
        for j in step:
            inside(peers[j])

    for step in back:
        arrive_and_inside(step)

    each_group(slots, lambda copy: copy.wait_recv())
    carried = []
    for m in range(slots):
        each_group(m, lambda copy: copy.wait_recv())

        def carry(g, before, m=m):
            added = total_buf[g, m * half : (m + 1) * half, :].astype(jnp.float32)
            new = keep_buf[g, m : m + 1, :] * before + added
            return jnp.where(g < group, new, before)

        carried.append(
            lax.fori_loop(
                0, groups, carry, jnp.zeros((half, 128), jnp.float32), unroll=groups <= 8
            )
        )
    gain = gain_buf[rank]

    def give_back(j):
        return pltpu.make_async_remote_copy(
            src_ref=send_buf.at[peers[j]],
            dst_ref=columns(out_ref, rank),
            send_sem=out_send.at[j],
            recv_sem=out_recv.at[j],
            device_id=devices[j],
            device_id_type=MESH,
        )

    def finish(i):
        state = jnp.concatenate(
            [
                t_buf[i, m * half : (m + 1) * half, :]
                + pre_buf[i, m : m + 1, :] * carried[m]
                for m in range(slots)
            ],
            axis=0,
        )
        read = mm(state.astype(jnp.bfloat16), split(qbuf[i], 0), NT)
        level = jnp.concatenate(
            [weight * jnp.exp(cumul) for cumul, weight in factors(i)], axis=1
        )
        total = inner_buf[i]
        for m in range(slots):
            total = total + level[m : m + 1, :] * read[m * half : (m + 1) * half, :]
        scale = lax.rsqrt(jnp.mean(total * total, axis=0, keepdims=True) + 1e-06)
        normed = total * scale
        flat = jnp.concatenate([normed[:, :tok], normed[:, tok:]], axis=0)
        send_buf[i] = (flat.T * gain).astype(jnp.bfloat16)

    for step in back:
        for j in step:
            finish(peers[j])
        for j in step:
            if j > 0:
                give_back(j).start()

    keep_own = pltpu.make_async_copy(
        send_buf.at[rank], columns(out_ref, rank), own_sem.at[0]
    )
    keep_own.start()

    for j in range(1, GROUP):
        for kind in range(3):
            transfer(kind, j).wait_send()
        copy = give_back(j)
        copy.wait_send()
        copy.wait_recv()

    for part in range(slots + 1):
        each_group(part, lambda copy: copy.wait_send())
    keep_own.wait()


def on_device(queries, key_vectors, value_vectors, log_decay, routes, route_weight, out_gain):
    n_ctx, n_mem = lax.axis_size("ctx"), lax.axis_size("mem")
    tok, width = queries.shape
    heads = log_decay.shape[1]
    groups = n_ctx * n_mem // GROUP
    slots = n_mem + 1
    pad = (slots + 9) // 8 * 8
    gain = out_gain.reshape(GROUP, 1, 128)
    hbm = pl.BlockSpec(memory_space=pltpu.HBM)
    return pl.pallas_call(
        functools.partial(kernel, n_ctx, n_mem, heads, pad),
        out_shape=jax.ShapeDtypeStruct((tok, width), jnp.bfloat16),
        in_specs=[hbm] * 7,
        out_specs=hbm,
        scratch_shapes=[
            pltpu.VMEM((GROUP, tok, 128), jnp.bfloat16),
            pltpu.VMEM((GROUP, 2, tok, 128), jnp.bfloat16),
            pltpu.VMEM((GROUP, tok, 128), jnp.bfloat16),
            pltpu.VMEM((GROUP, 2, tok, 128), jnp.bfloat16),
            pltpu.VMEM((GROUP, pad, tok), jnp.float32),
            pltpu.VMEM((GROUP, pad, tok), jnp.float32),
            pltpu.VMEM((GROUP, 2 * pad, tok), jnp.float32),
            pltpu.VMEM((GROUP, 128, tok), jnp.bfloat16),
            pltpu.VMEM((GROUP, slots * 64, 128), jnp.float32),
            pltpu.VMEM((GROUP, pad, 128), jnp.float32),
            pltpu.VMEM((GROUP, pad, 128), jnp.float32),
            pltpu.VMEM((GROUP, 64, 2 * tok), jnp.float32),
            pltpu.VMEM((GROUP, tok, 128), jnp.bfloat16),
            pltpu.VMEM((groups, slots * 64, 128), jnp.bfloat16),
            pltpu.VMEM((groups, pad, 128), jnp.float32),
            pltpu.VMEM((heads, tok), jnp.bfloat16),
            pltpu.VMEM((2, tok), jnp.int32),
            pltpu.VMEM((2, tok), jnp.float32),
            pltpu.VMEM((GROUP, 1, 128), jnp.float32),
            pltpu.SemaphoreType.DMA((3, GROUP)),
            pltpu.SemaphoreType.DMA((3, GROUP)),
            pltpu.SemaphoreType.DMA((GROUP,)),
            pltpu.SemaphoreType.DMA((GROUP,)),
            pltpu.SemaphoreType.DMA((slots + 1, groups)),
            pltpu.SemaphoreType.DMA((slots + 1, groups)),
            pltpu.SemaphoreType.DMA((1,)),
            pltpu.SemaphoreType.DMA((4,)),
            pltpu.SemaphoreType.DMA((3, GROUP)),
        ],
        compiler_params=pltpu.CompilerParams(
            collective_id=0, has_side_effects=True, vmem_limit_bytes=63 * 1024 * 1024
        ),
        cost_estimate=pl.CostEstimate(
            flops=2 * GROUP * 128 * 128 * 128 * 20, bytes_accessed=4 << 20, transcendentals=0
        ),
    )(queries, key_vectors, value_vectors, log_decay.T, routes.T, route_weight.T, gain)


def solution(mesh):
    rows = P(("ctx", "mem"), None)
    return jax.shard_map(
        on_device,
        mesh=mesh,
        in_specs=(rows, rows, rows, rows, rows, rows, P()),
        out_specs=rows,
        check_vma=False,
    )
```

```python
import functools

import jax
import jax.numpy as jnp
from jax import lax
from jax.experimental import pallas as pl
from jax.experimental.pallas import tpu as pltpu
from jax.sharding import PartitionSpec as P

MESH = pl.DeviceIdType.MESH
GROUP = 8
NT = (((1,), (1,)), ((), ()))
TN = (((0,), (0,)), ((), ()))


def mm(a, b, dims=(((1,), (0,)), ((), ()))):
    return lax.dot_general(a, b, dims, preferred_element_type=jnp.float32)


def halves(x):
    high = x.astype(jnp.bfloat16)
    return high, (x - high.astype(jnp.float32)).astype(jnp.bfloat16)


def kernel(
    n_ctx, n_mem, n_heads, pad,
    q_ref, k_ref, v_ref, decay_ref, routes_ref, weight_ref, gain_ref, out_ref,
    qbuf, kvbuf, q_mine, kv_mine, tab_mine, tab, cum_buf, vt_buf, t_buf, fade_buf, pre_buf, inner_buf, send_buf,
    total_buf, keep_buf, decay_buf, routes_buf, weight_buf, gain_buf,
    send_sem, recv_sem, out_send, out_recv, tot_send, tot_recv, own_sem, small_sem, stage_sem,
):
    slots = n_mem + 1
    groups = n_ctx * n_mem // GROUP
    tok = q_ref.shape[0]
    half = 64
    me = lax.axis_index("ctx") * n_mem + lax.axis_index("mem")
    group = lax.div(me, GROUP)
    rank = lax.rem(me, GROUP)

    def device(block):
        return (lax.div(block, n_mem), lax.rem(block, n_mem))

    def flipped(j):
        partner = rank
        for bit in (1, 2, 4):
            if j & bit:
                partner = partner + bit - 2 * bit * lax.rem(lax.div(rank, bit), 2)
        return partner

    peers = [flipped(j) for j in range(GROUP)]
    devices = [device(group * GROUP + r) for r in peers]

    def other(j):
        return lax.rem(group + j, groups)

    barrier = pltpu.get_barrier_semaphore()
    for j in range(1, GROUP):
        pl.semaphore_signal(barrier, inc=1, device_id=devices[j], device_id_type=MESH)

    def greet_group(j, _):
        pl.semaphore_signal(
            barrier, inc=1, device_id=device(other(j) * GROUP + rank), device_id_type=MESH
        )
        return 0

    lax.fori_loop(1, groups, greet_group, 0)

    small = [
        pltpu.make_async_copy(src, dst, small_sem.at[i])
        for i, (src, dst) in enumerate(
            (
                (decay_ref, decay_buf),
                (routes_ref, routes_buf),
                (weight_ref, weight_buf),
                (gain_ref, gain_buf),
            )
        )
    ]
    for copy in small:
        copy.start()

    def columns(ref, r):
        return ref.at[:, pl.ds(pl.multiple_of(r * 128, 128), 128)]

    send_order = (4, 2, 1, 6, 5, 3, 7)
    back = ((2, 6), (3, 7), (1, 5), (4, 0))

    def stage(kind, j):
        src = columns((k_ref, v_ref, q_ref)[kind], peers[j])
        if kind == 2:
            dst = qbuf.at[rank] if j == 0 else q_mine.at[peers[j]]
        else:
            dst = kvbuf.at[rank, kind] if j == 0 else kv_mine.at[peers[j], kind]
        return pltpu.make_async_copy(src, dst, stage_sem.at[kind, j])

    for j in send_order + (0,):
        for kind in range(2):
            stage(kind, j).start()

    row = lax.broadcasted_iota(jnp.int32, (tok, tok), 0)
    col = lax.broadcasted_iota(jnp.int32, (tok, tok), 1)
    causal = row <= col
    upper = jnp.where(causal, 1.0, 0.0).astype(jnp.bfloat16)
    for copy in small:
        copy.wait()
    decay = decay_buf[...].astype(jnp.float32)
    first, second = routes_buf[0:1, :], routes_buf[1:2, :]
    w_first, w_second = weight_buf[0:1, :], weight_buf[1:2, :]
    weights = [jnp.ones_like(w_first)] + [
        jnp.where(first == m, w_first, jnp.where(second == m, w_second, 0.0))
        for m in range(n_mem)
    ]
    tab_mine[...] = jnp.zeros_like(tab_mine)
    for p in range(GROUP):
        for m in range(slots):
            tab_mine[p, m : m + 1, :] = weights[m]
        tab_mine[p, slots : slots + 2, :] = decay[2 * p : 2 * p + 2, :]

    pl.semaphore_wait(barrier, GROUP - 1 + groups - 1)

    def transfer(kind, j):
        to = peers[j]
        src, dst = (
            (tab_mine.at[to], tab.at[rank]),
            (kv_mine.at[to], kvbuf.at[rank]),
            (q_mine.at[to], qbuf.at[rank]),
        )[kind]
        return pltpu.make_async_remote_copy(
            src_ref=src,
            dst_ref=dst,
            send_sem=send_sem.at[kind, j],
            recv_sem=recv_sem.at[kind, j],
            device_id=devices[j],
            device_id_type=MESH,
        )

    for j in send_order:
        transfer(0, j).start()
        for kind in range(2):
            stage(kind, j).wait()
        transfer(1, j).start()
    for step in back:
        for j in step:
            stage(2, j).start()
    for step in back:
        for j in step:
            if j > 0:
                stage(2, j).wait()
                transfer(2, j).start()

    tab[rank] = tab_mine[rank]

    left = lax.broadcasted_iota(jnp.int32, (1, 128), 1) < half

    def split(x, axis):
        zero = jnp.zeros_like(x)
        return jnp.concatenate([jnp.where(left, x, zero), jnp.where(left, zero, x)], axis=axis)

    def factors(i):
        weight = tab[i]
        return [(cum_buf[i, h * pad : (h + 1) * pad, :], weight) for h in range(2)]

    steps = ((0, 4), (2, 1), (6, 5), (3, 7))

    def gather_state(i):
        member = tab[i] > 0.0
        masked = [
            jnp.where(member, tab[i, slots + h : slots + h + 1, :], 0.0) for h in range(2)
        ]
        cum_buf[i] = mm(jnp.concatenate(masked, axis=0).astype(jnp.bfloat16), upper)
        vt = kvbuf[i, 1].astype(jnp.float32).T
        vt_buf[i] = vt.astype(jnp.bfloat16)
        parts, fades = [], []
        for h, (cumul, weight) in enumerate(factors(i)):
            last = cumul[:, tok - 1 : tok]
            faded = jnp.where(weight > 0.0, jnp.exp(last - cumul), 0.0)
            mine = vt[h * half : (h + 1) * half, :]
            parts.append(
                jnp.concatenate([mine * faded[m : m + 1, :] for m in range(slots)], axis=0)
            )
            fades.append(jnp.broadcast_to(jnp.exp(last), (pad, 128)))
        scaled = jnp.concatenate(parts, axis=1).astype(jnp.bfloat16)
        t_buf[i] = mm(scaled, split(kvbuf[i, 0], 0))
        fade_buf[i] = jnp.where(left, fades[0], fades[1])

    for step in steps:
        for j in step:
            if j == 0:
                for kind in range(2):
                    stage(kind, 0).wait()
            else:
                for kind in range(2):
                    transfer(kind, j).wait_recv()
        for j in step:
            gather_state(peers[j])

    def exchange(j, part):
        if part == slots:
            mine = keep_buf.at[group]
        else:
            mine = total_buf.at[group, pl.ds(part * half, half)]
        return pltpu.make_async_remote_copy(
            src_ref=mine,
            dst_ref=mine,
            send_sem=tot_send.at[part, j],
            recv_sem=tot_recv.at[part, j],
            device_id=device(other(j) * GROUP + rank),
            device_id_type=MESH,
        )

    def each_group(part, act):
        def run(j, _):
            act(exchange(j, part))
            return 0

        lax.fori_loop(1, groups, run, 0)

    kept = jnp.ones((pad, 128), jnp.float32)
    for i in range(GROUP):
        pre_buf[i] = kept
        kept = kept * fade_buf[i]
    keep_buf[group] = kept
    each_group(slots, lambda copy: copy.start())
    for m in range(slots):
        rows = pl.ds(m * half, half)
        state = t_buf[0, rows, :]
        t_buf[0, rows, :] = jnp.zeros((half, 128), jnp.float32)
        for i in range(1, GROUP):
            added = t_buf[i, rows, :]
            t_buf[i, rows, :] = state
            state = fade_buf[i, m : m + 1, :] * state + added
        total_buf[group, rows, :] = state.astype(jnp.bfloat16)
        each_group(m, lambda copy: copy.start())

    def inside(i):
        scores = mm(kvbuf[i, 0], split(qbuf[i], 0), NT)
        for h, (cumul, weight) in enumerate(factors(i)):
            middle = 0.5 * cumul[:, tok - 1 : tok]
            read_hi, read_lo = halves(weight * jnp.exp(cumul - middle))
            write_hi, write_lo = halves(jnp.where(weight > 0.0, jnp.exp(middle - cumul), 0.0))
            factor = mm(
                jnp.concatenate([write_hi, write_lo, write_hi], axis=0),
                jnp.concatenate([read_hi, read_hi, read_lo], axis=0),
                TN,
            )
            part = scores[:, h * tok : (h + 1) * tok] * factor
            part = jnp.where(causal, part, 0.0).astype(jnp.bfloat16)
            inner_buf[i, :, h * tok : (h + 1) * tok] = mm(
                vt_buf[i, h * half : (h + 1) * half, :], part
            )

    def arrive_and_inside(step):
        for j in step:
            if j == 0:
                stage(2, 0).wait()
            else:
                transfer(2, j).wait_recv()
        for j in step:
            inside(peers[j])

    arrive_and_inside(back[0])

    each_group(slots, lambda copy: copy.wait_recv())
    carried = []
    for m in range(slots):
        each_group(m, lambda copy: copy.wait_recv())

        def carry(g, before, m=m):
            added = total_buf[g, m * half : (m + 1) * half, :].astype(jnp.float32)
            new = keep_buf[g, m : m + 1, :] * before + added
            return jnp.where(g < group, new, before)

        carried.append(
            lax.fori_loop(
                0, groups, carry, jnp.zeros((half, 128), jnp.float32), unroll=groups <= 8
            )
        )
    gain = gain_buf[rank]

    def give_back(j):
        return pltpu.make_async_remote_copy(
            src_ref=send_buf.at[peers[j]],
            dst_ref=columns(out_ref, rank),
            send_sem=out_send.at[j],
            recv_sem=out_recv.at[j],
            device_id=devices[j],
            device_id_type=MESH,
        )

    def finish(i):
        state = jnp.concatenate(
            [
                t_buf[i, m * half : (m + 1) * half, :]
                + pre_buf[i, m : m + 1, :] * carried[m]
                for m in range(slots)
            ],
            axis=0,
        )
        read = mm(state.astype(jnp.bfloat16), split(qbuf[i], 0), NT)
        level = jnp.concatenate(
            [weight * jnp.exp(cumul) for cumul, weight in factors(i)], axis=1
        )
        total = inner_buf[i]
        for m in range(slots):
            total = total + level[m : m + 1, :] * read[m * half : (m + 1) * half, :]
        scale = lax.rsqrt(jnp.mean(total * total, axis=0, keepdims=True) + 1e-06)
        normed = total * scale
        flat = jnp.concatenate([normed[:, :tok], normed[:, tok:]], axis=0)
        send_buf[i] = (flat.T * gain).astype(jnp.bfloat16)

    for number, step in enumerate(back):
        if number > 0:
            arrive_and_inside(step)
        for j in step:
            finish(peers[j])
        for j in step:
            if j > 0:
                give_back(j).start()

    keep_own = pltpu.make_async_copy(
        send_buf.at[rank], columns(out_ref, rank), own_sem.at[0]
    )
    keep_own.start()

    for j in range(1, GROUP):
        for kind in range(3):
            transfer(kind, j).wait_send()
        copy = give_back(j)
        copy.wait_send()
        copy.wait_recv()

    for part in range(slots + 1):
        each_group(part, lambda copy: copy.wait_send())
    keep_own.wait()


def on_device(queries, key_vectors, value_vectors, log_decay, routes, route_weight, out_gain):
    n_ctx, n_mem = lax.axis_size("ctx"), lax.axis_size("mem")
    tok, width = queries.shape
    heads = log_decay.shape[1]
    groups = n_ctx * n_mem // GROUP
    slots = n_mem + 1
    pad = (slots + 9) // 8 * 8
    gain = out_gain.reshape(GROUP, 1, 128)
    hbm = pl.BlockSpec(memory_space=pltpu.HBM)
    return pl.pallas_call(
        functools.partial(kernel, n_ctx, n_mem, heads, pad),
        out_shape=jax.ShapeDtypeStruct((tok, width), jnp.bfloat16),
        in_specs=[hbm] * 7,
        out_specs=hbm,
        scratch_shapes=[
            pltpu.VMEM((GROUP, tok, 128), jnp.bfloat16),
            pltpu.VMEM((GROUP, 2, tok, 128), jnp.bfloat16),
            pltpu.VMEM((GROUP, tok, 128), jnp.bfloat16),
            pltpu.VMEM((GROUP, 2, tok, 128), jnp.bfloat16),
            pltpu.VMEM((GROUP, pad, tok), jnp.float32),
            pltpu.VMEM((GROUP, pad, tok), jnp.float32),
            pltpu.VMEM((GROUP, 2 * pad, tok), jnp.float32),
            pltpu.VMEM((GROUP, 128, tok), jnp.bfloat16),
            pltpu.VMEM((GROUP, slots * 64, 128), jnp.float32),
            pltpu.VMEM((GROUP, pad, 128), jnp.float32),
            pltpu.VMEM((GROUP, pad, 128), jnp.float32),
            pltpu.VMEM((GROUP, 64, 2 * tok), jnp.float32),
            pltpu.VMEM((GROUP, tok, 128), jnp.bfloat16),
            pltpu.VMEM((groups, slots * 64, 128), jnp.bfloat16),
            pltpu.VMEM((groups, pad, 128), jnp.float32),
            pltpu.VMEM((heads, tok), jnp.bfloat16),
            pltpu.VMEM((2, tok), jnp.int32),
            pltpu.VMEM((2, tok), jnp.float32),
            pltpu.VMEM((GROUP, 1, 128), jnp.float32),
            pltpu.SemaphoreType.DMA((3, GROUP)),
            pltpu.SemaphoreType.DMA((3, GROUP)),
            pltpu.SemaphoreType.DMA((GROUP,)),
            pltpu.SemaphoreType.DMA((GROUP,)),
            pltpu.SemaphoreType.DMA((slots + 1, groups)),
            pltpu.SemaphoreType.DMA((slots + 1, groups)),
            pltpu.SemaphoreType.DMA((1,)),
            pltpu.SemaphoreType.DMA((4,)),
            pltpu.SemaphoreType.DMA((3, GROUP)),
        ],
        compiler_params=pltpu.CompilerParams(
            collective_id=0, has_side_effects=True, vmem_limit_bytes=63 * 1024 * 1024
        ),
        cost_estimate=pl.CostEstimate(
            flops=2 * GROUP * 128 * 128 * 128 * 20, bytes_accessed=4 << 20, transcendentals=0
        ),
    )(queries, key_vectors, value_vectors, log_decay.T, routes.T, route_weight.T, gain)


def solution(mesh):
    rows = P(("ctx", "mem"), None)
    return jax.shard_map(
        on_device,
        mesh=mesh,
        in_specs=(rows, rows, rows, rows, rows, rows, P()),
        out_specs=rows,
        check_vma=False,
    )
```

```python
import functools

import jax
import jax.numpy as jnp
from jax import lax
from jax.experimental import pallas as pl
from jax.experimental.pallas import tpu as pltpu
from jax.sharding import PartitionSpec as P

MESH = pl.DeviceIdType.MESH
GROUP = 8
PIECES = 8
NT = (((1,), (1,)), ((), ()))
TN = (((0,), (0,)), ((), ()))


def mm(a, b, dims=(((1,), (0,)), ((), ()))):
    return lax.dot_general(a, b, dims, preferred_element_type=jnp.float32)


def halves(x):
    high = x.astype(jnp.bfloat16)
    return high, (x - high.astype(jnp.float32)).astype(jnp.bfloat16)


def kernel(
    n_ctx, n_mem, n_heads, pad,
    q_ref, k_ref, v_ref, decay_ref, routes_ref, weight_ref, gain_ref, out_ref,
    qbuf, kvbuf, q_mine, kv_mine, tab_mine, tab, cum_buf, vt_buf, t_buf, fade_buf, pre_buf, inner_buf, send_buf,
    total_buf, keep_buf, decay_buf, routes_buf, weight_buf, gain_buf,
    send_sem, recv_sem, out_send, out_recv, tot_send, tot_recv, own_sem, small_sem, stage_sem,
):
    slots = n_mem + 1
    groups = n_ctx * n_mem // GROUP
    tok = q_ref.shape[0]
    half = 64
    me = lax.axis_index("ctx") * n_mem + lax.axis_index("mem")
    group = lax.div(me, GROUP)
    rank = lax.rem(me, GROUP)

    def device(block):
        return (lax.div(block, n_mem), lax.rem(block, n_mem))

    def flipped(j):
        partner = rank
        for bit in (1, 2, 4):
            if j & bit:
                partner = partner + bit - 2 * bit * lax.rem(lax.div(rank, bit), 2)
        return partner

    peers = [flipped(j) for j in range(GROUP)]
    devices = [device(group * GROUP + r) for r in peers]

    def other(j):
        return lax.rem(group + j, groups)

    barrier = pltpu.get_barrier_semaphore()
    for j in range(1, GROUP):
        pl.semaphore_signal(barrier, inc=1, device_id=devices[j], device_id_type=MESH)

    def greet_group(j, _):
        pl.semaphore_signal(
            barrier, inc=1, device_id=device(other(j) * GROUP + rank), device_id_type=MESH
        )
        return 0

    lax.fori_loop(1, groups, greet_group, 0)

    small = [
        pltpu.make_async_copy(src, dst, small_sem.at[i])
        for i, (src, dst) in enumerate(
            (
                (decay_ref, decay_buf),
                (routes_ref, routes_buf),
                (weight_ref, weight_buf),
                (gain_ref, gain_buf),
            )
        )
    ]
    for copy in small:
        copy.start()

    def columns(ref, r):
        return ref.at[:, pl.ds(pl.multiple_of(r * 128, 128), 128)]

    send_order = (4, 2, 1, 6, 5, 3, 7)
    back = ((4, 0), (2, 6), (3, 7), (1, 5))

    def stage(kind, j):
        src = columns((k_ref, v_ref, q_ref)[kind], peers[j])
        if kind == 2:
            dst = qbuf.at[rank] if j == 0 else q_mine.at[peers[j]]
        else:
            dst = kvbuf.at[rank, kind] if j == 0 else kv_mine.at[peers[j], kind]
        return pltpu.make_async_copy(src, dst, stage_sem.at[kind, j])

    for j in send_order + (0,):
        for kind in range(2):
            stage(kind, j).start()

    row = lax.broadcasted_iota(jnp.int32, (tok, tok), 0)
    col = lax.broadcasted_iota(jnp.int32, (tok, tok), 1)
    causal = row <= col
    upper = jnp.where(causal, 1.0, 0.0).astype(jnp.bfloat16)
    for copy in small:
        copy.wait()
    decay = decay_buf[...].astype(jnp.float32)
    first, second = routes_buf[0:1, :], routes_buf[1:2, :]
    w_first, w_second = weight_buf[0:1, :], weight_buf[1:2, :]
    weights = [jnp.ones_like(w_first)] + [
        jnp.where(first == m, w_first, jnp.where(second == m, w_second, 0.0))
        for m in range(n_mem)
    ]
    tab_mine[...] = jnp.zeros_like(tab_mine)
    for p in range(GROUP):
        for m in range(slots):
            tab_mine[p, m : m + 1, :] = weights[m]
        tab_mine[p, slots : slots + 2, :] = decay[2 * p : 2 * p + 2, :]

    pl.semaphore_wait(barrier, GROUP - 1 + groups - 1)

    def transfer(kind, j):
        to = peers[j]
        src, dst = (
            (tab_mine.at[to], tab.at[rank]),
            (kv_mine.at[to], kvbuf.at[rank]),
            (q_mine.at[to], qbuf.at[rank]),
        )[kind]
        return pltpu.make_async_remote_copy(
            src_ref=src,
            dst_ref=dst,
            send_sem=send_sem.at[kind, j],
            recv_sem=recv_sem.at[kind, j],
            device_id=devices[j],
            device_id_type=MESH,
        )

    for j in send_order:
        transfer(0, j).start()
        for kind in range(2):
            stage(kind, j).wait()
        transfer(1, j).start()
    for step in back:
        for j in step:
            stage(2, j).start()
    for step in back:
        for j in step:
            if j > 0:
                stage(2, j).wait()
                transfer(2, j).start()

    tab[rank] = tab_mine[rank]

    left = lax.broadcasted_iota(jnp.int32, (1, 128), 1) < half

    def split(x, axis):
        zero = jnp.zeros_like(x)
        return jnp.concatenate([jnp.where(left, x, zero), jnp.where(left, zero, x)], axis=axis)

    def factors(i):
        weight = tab[i]
        return [(cum_buf[i, h * pad : (h + 1) * pad, :], weight) for h in range(2)]

    steps = ((0, 4), (2, 1), (6, 5), (3, 7))

    def gather_state(i):
        member = tab[i] > 0.0
        masked = [
            jnp.where(member, tab[i, slots + h : slots + h + 1, :], 0.0) for h in range(2)
        ]
        cum_buf[i] = mm(jnp.concatenate(masked, axis=0).astype(jnp.bfloat16), upper)
        vt = kvbuf[i, 1].astype(jnp.float32).T
        vt_buf[i] = vt.astype(jnp.bfloat16)
        parts, fades = [], []
        for h, (cumul, weight) in enumerate(factors(i)):
            last = cumul[:, tok - 1 : tok]
            faded = jnp.where(weight > 0.0, jnp.exp(last - cumul), 0.0)
            mine = vt[h * half : (h + 1) * half, :]
            parts.append(
                jnp.concatenate([mine * faded[m : m + 1, :] for m in range(slots)], axis=0)
            )
            fades.append(jnp.broadcast_to(jnp.exp(last), (pad, 128)))
        scaled = jnp.concatenate(parts, axis=1).astype(jnp.bfloat16)
        t_buf[i] = mm(scaled, split(kvbuf[i, 0], 0))
        fade_buf[i] = jnp.where(left, fades[0], fades[1])

    for step in steps:
        for j in step:
            if j == 0:
                for kind in range(2):
                    stage(kind, 0).wait()
            else:
                for kind in range(2):
                    transfer(kind, j).wait_recv()
        for j in step:
            gather_state(peers[j])

    def exchange(j, part):
        if part == slots:
            mine = keep_buf.at[group]
        else:
            mine = total_buf.at[group, pl.ds(part * half, half)]
        return pltpu.make_async_remote_copy(
            src_ref=mine,
            dst_ref=mine,
            send_sem=tot_send.at[part, j],
            recv_sem=tot_recv.at[part, j],
            device_id=device(other(j) * GROUP + rank),
            device_id_type=MESH,
        )

    def each_group(part, act):
        def run(j, _):
            act(exchange(j, part))
            return 0

        lax.fori_loop(1, groups, run, 0)

    kept = jnp.ones((pad, 128), jnp.float32)
    for i in range(GROUP):
        pre_buf[i] = kept
        kept = kept * fade_buf[i]
    keep_buf[group] = kept
    each_group(slots, lambda copy: copy.start())
    for m in range(slots):
        rows = pl.ds(m * half, half)
        state = t_buf[0, rows, :]
        t_buf[0, rows, :] = jnp.zeros((half, 128), jnp.float32)
        for i in range(1, GROUP):
            added = t_buf[i, rows, :]
            t_buf[i, rows, :] = state
            state = fade_buf[i, m : m + 1, :] * state + added
        total_buf[group, rows, :] = state.astype(jnp.bfloat16)
        each_group(m, lambda copy: copy.start())

    def inside(i):
        scores = mm(kvbuf[i, 0], split(qbuf[i], 0), NT)
        for h, (cumul, weight) in enumerate(factors(i)):
            middle = 0.5 * cumul[:, tok - 1 : tok]
            read_hi, read_lo = halves(weight * jnp.exp(cumul - middle))
            write_hi, write_lo = halves(jnp.where(weight > 0.0, jnp.exp(middle - cumul), 0.0))
            factor = mm(
                jnp.concatenate([write_hi, write_lo, write_hi], axis=0),
                jnp.concatenate([read_hi, read_hi, read_lo], axis=0),
                TN,
            )
            part = scores[:, h * tok : (h + 1) * tok] * factor
            part = jnp.where(causal, part, 0.0).astype(jnp.bfloat16)
            inner_buf[i, :, h * tok : (h + 1) * tok] = mm(
                vt_buf[i, h * half : (h + 1) * half, :], part
            )

    def arrive_and_inside(step):
        for j in step:
            if j == 0:
                stage(2, 0).wait()
            else:
                transfer(2, j).wait_recv()
        for j in step:
            inside(peers[j])

    arrive_and_inside(back[0])

    each_group(slots, lambda copy: copy.wait_recv())
    carried = []
    for m in range(slots):
        each_group(m, lambda copy: copy.wait_recv())

        def carry(g, before, m=m):
            added = total_buf[g, m * half : (m + 1) * half, :].astype(jnp.float32)
            new = keep_buf[g, m : m + 1, :] * before + added
            return jnp.where(g < group, new, before)

        carried.append(
            lax.fori_loop(
                0, groups, carry, jnp.zeros((half, 128), jnp.float32), unroll=groups <= 8
            )
        )
    gain = gain_buf[rank]

    def give_back(j):
        return pltpu.make_async_remote_copy(
            src_ref=send_buf.at[peers[j]],
            dst_ref=columns(out_ref, rank),
            send_sem=out_send.at[j],
            recv_sem=out_recv.at[j],
            device_id=devices[j],
            device_id_type=MESH,
        )

    def finish(i):
        state = jnp.concatenate(
            [
                t_buf[i, m * half : (m + 1) * half, :]
                + pre_buf[i, m : m + 1, :] * carried[m]
                for m in range(slots)
            ],
            axis=0,
        )
        read = mm(state.astype(jnp.bfloat16), split(qbuf[i], 0), NT)
        level = jnp.concatenate(
            [weight * jnp.exp(cumul) for cumul, weight in factors(i)], axis=1
        )
        total = inner_buf[i]
        for m in range(slots):
            total = total + level[m : m + 1, :] * read[m * half : (m + 1) * half, :]
        scale = lax.rsqrt(jnp.mean(total * total, axis=0, keepdims=True) + 1e-06)
        normed = total * scale
        flat = jnp.concatenate([normed[:, :tok], normed[:, tok:]], axis=0)
        send_buf[i] = (flat.T * gain).astype(jnp.bfloat16)

    for number, step in enumerate(back):
        if number > 0:
            arrive_and_inside(step)
        for j in step:
            finish(peers[j])
        for j in step:
            if j > 0:
                give_back(j).start()

    keep_own = pltpu.make_async_copy(
        send_buf.at[rank], columns(out_ref, rank), own_sem.at[0]
    )
    keep_own.start()

    for j in range(1, GROUP):
        for kind in range(3):
            transfer(kind, j).wait_send()
        copy = give_back(j)
        copy.wait_send()
        copy.wait_recv()

    for part in range(slots + 1):
        each_group(part, lambda copy: copy.wait_send())
    keep_own.wait()


def hand_over(src_ref, dst_ref, sem):
    rows = src_ref.shape[0] // PIECES
    copies = [
        pltpu.make_async_copy(
            src_ref.at[pl.ds(i * rows, rows)], dst_ref.at[pl.ds(i * rows, rows)], sem.at[i]
        )
        for i in range(PIECES)
    ]
    for copy in copies:
        copy.start()
    for copy in copies:
        copy.wait()


def on_device(queries, key_vectors, value_vectors, log_decay, routes, route_weight, out_gain):
    n_ctx, n_mem = lax.axis_size("ctx"), lax.axis_size("mem")
    tok, width = queries.shape
    heads = log_decay.shape[1]
    groups = n_ctx * n_mem // GROUP
    slots = n_mem + 1
    pad = (slots + 9) // 8 * 8
    gain = out_gain.reshape(GROUP, 1, 128)
    hbm = pl.BlockSpec(memory_space=pltpu.HBM)
    mixed = pl.pallas_call(
        functools.partial(kernel, n_ctx, n_mem, heads, pad),
        out_shape=jax.ShapeDtypeStruct((tok, width), jnp.bfloat16),
        in_specs=[hbm] * 7,
        out_specs=hbm,
        scratch_shapes=[
            pltpu.VMEM((GROUP, tok, 128), jnp.bfloat16),
            pltpu.VMEM((GROUP, 2, tok, 128), jnp.bfloat16),
            pltpu.VMEM((GROUP, tok, 128), jnp.bfloat16),
            pltpu.VMEM((GROUP, 2, tok, 128), jnp.bfloat16),
            pltpu.VMEM((GROUP, pad, tok), jnp.float32),
            pltpu.VMEM((GROUP, pad, tok), jnp.float32),
            pltpu.VMEM((GROUP, 2 * pad, tok), jnp.float32),
            pltpu.VMEM((GROUP, 128, tok), jnp.bfloat16),
            pltpu.VMEM((GROUP, slots * 64, 128), jnp.float32),
            pltpu.VMEM((GROUP, pad, 128), jnp.float32),
            pltpu.VMEM((GROUP, pad, 128), jnp.float32),
            pltpu.VMEM((GROUP, 64, 2 * tok), jnp.float32),
            pltpu.VMEM((GROUP, tok, 128), jnp.bfloat16),
            pltpu.VMEM((groups, slots * 64, 128), jnp.bfloat16),
            pltpu.VMEM((groups, pad, 128), jnp.float32),
            pltpu.VMEM((heads, tok), jnp.bfloat16),
            pltpu.VMEM((2, tok), jnp.int32),
            pltpu.VMEM((2, tok), jnp.float32),
            pltpu.VMEM((GROUP, 1, 128), jnp.float32),
            pltpu.SemaphoreType.DMA((3, GROUP)),
            pltpu.SemaphoreType.DMA((3, GROUP)),
            pltpu.SemaphoreType.DMA((GROUP,)),
            pltpu.SemaphoreType.DMA((GROUP,)),
            pltpu.SemaphoreType.DMA((slots + 1, groups)),
            pltpu.SemaphoreType.DMA((slots + 1, groups)),
            pltpu.SemaphoreType.DMA((1,)),
            pltpu.SemaphoreType.DMA((4,)),
            pltpu.SemaphoreType.DMA((3, GROUP)),
        ],
        compiler_params=pltpu.CompilerParams(
            collective_id=0, has_side_effects=True, vmem_limit_bytes=63 * 1024 * 1024
        ),
        cost_estimate=pl.CostEstimate(
            flops=2 * GROUP * 128 * 128 * 128 * 20, bytes_accessed=4 << 20, transcendentals=0
        ),
    )(queries, key_vectors, value_vectors, log_decay.T, routes.T, route_weight.T, gain)
    return pl.pallas_call(
        hand_over,
        out_shape=jax.ShapeDtypeStruct((tok, width), jnp.bfloat16),
        in_specs=[hbm],
        out_specs=hbm,
        scratch_shapes=[pltpu.SemaphoreType.DMA((PIECES,))],
        compiler_params=pltpu.CompilerParams(vmem_limit_bytes=63 * 1024 * 1024),
    )(mixed)


def solution(mesh):
    rows = P(("ctx", "mem"), None)
    return jax.shard_map(
        on_device,
        mesh=mesh,
        in_specs=(rows, rows, rows, rows, rows, rows, P()),
        out_specs=rows,
        check_vma=False,
    )
```
